32 devices in a mesh: ublk: 8 (over z, x), salt: 4 (over y, core).
Axes of the slice: x: 2, y: 2, z: 4, core: 2. Of those that a mesh axis runs over, the one named last changes fastest.
Arguments:
- user_factors: bfloat16 [8, 4096, 256], P('ublk', 'salt')
- tile_users: int32 [8, 4, 4096], P('ublk', 'salt'), may hold values from 0 to 4095
- tile_items: int32 [8, 4, 4096], P('ublk', 'salt'), may hold values from 0 to 255
- tile_weight: float32 [8, 4, 4096], P('ublk', 'salt'), may hold values from 0.5 to 8
- live_count: int32 [8, 4], P('ublk', 'salt'), may hold values from 2048 to 4096, as said below
Outputs:
- item_factors: float32 [4, 256, 256], P('salt', 'ublk')
- residual: float32 [4, 256, 256], P('salt', 'ublk')
The draws below stay inside these ranges and needn't reach their ends.
Inputs may be any that keep to these rules, and one draw needn't show every extreme that they name: Every entry of live_count is at least 2048 and at most 4096; some tile is full.
All inputs are finite; a program needn't handle non-finite values.
Results may differ from the reference program's by a relative error of at most 0.0022.
Values may be sent and summed in bfloat16 or wider, within the bound.
No kernel may reach another device: no remote copies, remote signals or barrier semaphores. Data moves between devices by JAX's collectives and lax.ppermute only.
A program may use at most 64 MiB of HBM per device.

```python
import math
import jax
import jax.numpy as jnp
import numpy as np
from jax import lax

K = 256
ITERS = 8
NNZ_DEV = 4096
USER_BLK = 4096
ITEM_SALT = 256
N_UBLK = 8
N_SALT = 4


def draw_user_factors(key, part):
    key_cols, key_rows, key_base = jax.random.split(key, 3)
    cols = jnp.exp(jax.random.uniform(key_cols, (K,), jnp.float32, math.log(0.3), 0.0))
    scales = jnp.exp(jax.random.uniform(key_rows, (N_UBLK, USER_BLK, 1), jnp.float32, math.log(0.3), math.log(3.0)))
    base = jax.random.normal(key_base, (N_UBLK, USER_BLK, K), jnp.float32)
    values = base * cols * scales / jnp.sqrt(jnp.float32(N_UBLK * USER_BLK))
    return values.astype(jnp.bfloat16)


def draw_live_count(key, part):
    key_counts, key_full = jax.random.split(jax.random.fold_in(key, 17))
    counts = jax.random.randint(key_counts, (N_UBLK * N_SALT,), NNZ_DEV // 2, NNZ_DEV + 1)
    chosen = jax.random.randint(key_full, (), 0, N_UBLK * N_SALT)
    positions = jnp.arange(N_UBLK * N_SALT)
    counts = jnp.where(positions == chosen, NNZ_DEV, counts)
    return counts.reshape(N_UBLK, N_SALT).astype(jnp.int32)


def place_ends(result, own_key, smallest, top_value):
    extent = result.shape
    index_at = [jax.random.randint(jax.random.fold_in(own_key, axis), (), 0, extent[axis]) for axis in range(len(extent))]
    result = result.at[tuple(index_at)].set(smallest)
    longest = extent.index(max(extent))
    index_at[longest] = (index_at[longest] + 1) % extent[longest]
    return result.at[tuple(index_at)].set(top_value)


def levels(stream_key, shape, cuts, smallest, high):
    gain = 1.0
    for axis_at, shards_of in cuts:
        heights = jax.random.uniform(jax.random.fold_in(jax.random.fold_in(stream_key, 6), axis_at), (shards_of,), jnp.float32, smallest / len(cuts), high / len(cuts))
        gain = gain * jnp.repeat(jnp.exp(heights), shape[axis_at] // shards_of).reshape((-1,) + (1,) * (len(shape) - 1 - axis_at))
    return gain


def rank_bounds(amount, skew):
    portions = [(1 << 20) // math.isqrt(grade ** skew) + 1 for grade in range(1, amount + 1)]
    deviation = 1 + sum(portions) // (1 << 30)
    return np.cumsum(np.array([max(1, weight // deviation) for weight in portions]))


def ranked(stream_key, shape, number_of, lean):
    grid = rank_bounds(number_of, lean)
    ticket = jax.random.randint(jax.random.fold_in(stream_key, 1), shape, 0, int(grid[number_of - 1]))
    rank = jnp.searchsorted(jnp.asarray(grid, jnp.int32), ticket, side="right")
    return jax.random.permutation(jax.random.fold_in(stream_key, 2), number_of)[rank].astype(jnp.int32)


def setup_inputs(seed: int = 0) -> dict:
    keys = jax.random.split(jax.random.key(seed), 6)
    user_factors = draw_user_factors(jax.random.fold_in(keys[5], 71), 0)
    tile_users = place_ends(jax.random.randint(keys[1], (N_UBLK, N_SALT, NNZ_DEV), 0, USER_BLK), jax.random.fold_in(keys[1], 1), 0, USER_BLK - 1).astype(jnp.int32)
    tile_items = place_ends(ranked(keys[2], (N_UBLK, N_SALT, NNZ_DEV), ITEM_SALT, 2), jax.random.fold_in(keys[2], 3), 0, ITEM_SALT - 1).astype(jnp.int32)
    tile_weight = jnp.clip(jnp.exp(math.log(8.0) - 2.7725887 * jax.random.uniform(keys[3], (N_UBLK, N_SALT, NNZ_DEV), jnp.float32) ** levels(keys[3], (N_UBLK, N_SALT, NNZ_DEV), ((0, 8), (1, 4)), -0.2, 0.2)), 0.5, 8.0)
    live_count = draw_live_count(jax.random.fold_in(keys[5], 71), 0)
    return {"user_factors": user_factors, "tile_users": tile_users, "tile_items": tile_items, "tile_weight": tile_weight, "live_count": live_count}


REG = 1.0
EPS = 1e-6


def operate(direction, rows, items, weight, gram):
    along = jnp.sum(rows * direction[items], axis=1) * weight
    local = jax.ops.segment_sum(along[:, None] * rows, items, num_segments=direction.shape[0])
    return local + jnp.dot(direction, gram, precision=lax.Precision.HIGHEST) + REG * direction


def reference(user_factors, tile_users, tile_items, tile_weight, live_count):
    flat = user_factors.reshape(N_UBLK * USER_BLK, K)
    gram = jnp.dot(flat.T, flat, preferred_element_type=jnp.float32)
    offsets = (jnp.arange(N_UBLK) * USER_BLK).astype(jnp.int32)
    slots = jnp.arange(NNZ_DEV).astype(jnp.int32)
    solved = []
    leftover = []
    for column in range(N_SALT):
        users = (tile_users[:, column, :] + offsets[:, None]).reshape(-1)
        items = tile_items[:, column, :].reshape(-1)
        live = slots[None, :] < live_count[:, column][:, None]
        raw = tile_weight[:, column, :]
        weight = jnp.where(live, raw, jnp.zeros_like(raw)).reshape(-1)
        confid = jnp.where(live, 1.0 + raw, jnp.zeros_like(raw)).reshape(-1)
        rows = flat[users].astype(jnp.float32)
        rhs = jax.ops.segment_sum(confid[:, None] * rows, items, num_segments=ITEM_SALT)
        solution = jnp.zeros_like(rhs)
        resid = rhs
        direction = rhs
        norm_now = jnp.sum(resid * resid, axis=1)
        for step in range(ITERS):
            image = operate(direction, rows, items, weight, gram)
            alpha = norm_now / (jnp.sum(direction * image, axis=1) + EPS)
            solution = solution + alpha[:, None] * direction
            resid = resid - alpha[:, None] * image
            norm_next = jnp.sum(resid * resid, axis=1)
            direction = resid + (norm_next / (norm_now + EPS))[:, None] * direction
            norm_now = norm_next
        solved.append(solution)
        leftover.append(resid)
    return jnp.stack(solved), jnp.stack(leftover)
```

```python
import functools

import jax
import jax.numpy as jnp
from jax import lax
from jax.experimental import pallas as pl
from jax.experimental.pallas import tpu as pltpu
from jax.sharding import PartitionSpec as P

ITERS = 8
ITEM_DEV = 32

REG = 1.0
EPS = 1e-06

LANES = 128
STEP = 1024
TABLE_BYTES = 1 << 25


def conjugate(rhs, image_of):
    solution = jnp.zeros_like(rhs)
    resid = rhs
    direction = rhs
    norm_now = jnp.sum(resid * resid, axis=1)
    for step in range(ITERS):
        image = image_of(direction)
        alpha = norm_now / (jnp.sum(direction * image, axis=1) + EPS)
        solution = solution + alpha[:, None] * direction
        resid = resid - alpha[:, None] * image
        norm_next = jnp.sum(resid * resid, axis=1)
        direction = resid + (norm_next / (norm_now + EPS))[:, None] * direction
        norm_now = norm_next
    return (solution, resid)


def reduced_body(user_factors, tile_users, tile_items, tile_weight, live_count):
    shard = user_factors[0]
    block = lax.all_gather(shard, "salt", axis=0, tiled=True)
    contract = (((0,), (0,)), ((), ()))
    own_gram = lax.dot_general(block, block, contract, preferred_element_type=jnp.float32)
    gram = lax.psum(own_gram, "ublk")
    users = tile_users[0, 0]
    items = tile_items[0, 0]
    raw = tile_weight[0, 0]
    live = jnp.arange(users.shape[0], dtype=jnp.int32) < live_count[0, 0]
    weight = jnp.where(live, raw, jnp.zeros_like(raw))
    confid = jnp.where(live, 1.0 + raw, jnp.zeros_like(raw))
    rows = jnp.take(block, users, axis=0).astype(jnp.float32)
    column_items = ITEM_DEV * lax.axis_size("ublk")
    rhs_terms = jax.ops.segment_sum(confid[:, None] * rows, items, num_segments=column_items)

    def local_terms(whole_dir):
        along = jnp.sum(rows * whole_dir[items], axis=1) * weight
        return jax.ops.segment_sum(along[:, None] * rows, items, num_segments=column_items)

    def finish(summed, direction):
        return summed + jnp.dot(direction, gram, precision=lax.Precision.HIGHEST) + REG * direction

    rhs = lax.psum(rhs_terms, "ublk")

    def image_every(direction):
        summed = lax.psum(local_terms(direction), "ublk")
        return finish(summed, direction)

    solution_all, resid_all = conjugate(rhs, image_every)
    start = lax.axis_index("ublk") * ITEM_DEV
    solution = lax.dynamic_slice_in_dim(solution_all, start, ITEM_DEV, 0)
    resid = lax.dynamic_slice_in_dim(resid_all, start, ITEM_DEV, 0)
    return (solution[None], resid[None])


def two_parts(value):
    high = value.astype(jnp.bfloat16)
    low = (value - high.astype(jnp.float32)).astype(jnp.bfloat16)
    return jnp.concatenate([high, low], axis=0)


def pick_rows(block, lo, hi, tile, first_ref, last_ref, keys_ref, weight_ref, table, rows, item_s, weight_s, count, total):
    lane = lax.broadcasted_iota(jnp.int32, (LANES, LANES), 1)

    def group(j, carry):
        low = jnp.maximum(first_ref[block, j], lo)
        high = jnp.minimum(last_ref[block, j], hi - 1)

        @pl.when(low <= high)
        def _():
            at = count[0]
            key = keys_ref[0, pl.ds(j, 1), :]
            mine = (key >= lo) & (key < hi)
            place = key - lo
            user = jnp.where(mine, place // ITEM_DEV, -1)
            item_s[pl.ds(at, 1), :] = jnp.where(mine, place % ITEM_DEV, -1)
            weight_s[pl.ds(at, 1), :] = jnp.where(mine, weight_ref[0, pl.ds(j, 1), :], 0.0)
            down = jnp.transpose(jnp.broadcast_to(user.astype(jnp.float32), (LANES, LANES))).astype(jnp.int32)
            total[...] = jnp.zeros_like(total)

            def part(t, inner):
                start = pl.multiple_of(t * tile, tile)
                ahead = down - start
                hot = jnp.concatenate(
                    [(ahead == lane + LANES * q).astype(jnp.bfloat16) for q in range(tile // LANES)], axis=1
                )
                total[...] += jnp.dot(hot, table[pl.ds(start, tile), :], preferred_element_type=jnp.float32)
                return inner

            lax.fori_loop((low - lo) // (ITEM_DEV * tile), (high - lo) // (ITEM_DEV * tile) + 1, part, 0)
            rows[pl.ds(pl.multiple_of(at * LANES, LANES), LANES), :] = total[...].astype(rows.dtype)
            count[0] = at + 1

        return carry

    lax.fori_loop(0, first_ref.shape[1], group, 0)


def solve_items(rows, item_s, weight_s, count, gram, solution_ref, resid_ref):
    groups = STEP // LANES
    filled = count[0]
    steps = (filled + groups - 1) // groups
    for extra in range(groups - 1):
        at = filled + extra

        @pl.when(at < steps * groups)
        def _():
            rows[pl.ds(pl.multiple_of(at * LANES, LANES), LANES), :] = jnp.zeros((LANES, rows.shape[1]), rows.dtype)
            item_s[pl.ds(at, 1), :] = jnp.full((1, LANES), -1, jnp.int32)
            weight_s[pl.ds(at, 1), :] = jnp.zeros((1, LANES), jnp.float32)

    own = lax.broadcasted_iota(jnp.int32, (ITEM_DEV, STEP), 0)

    def along(ref, step):
        return jnp.concatenate([ref[pl.ds(step * groups + g, 1), :] for g in range(groups)], axis=1)

    def held(step):
        return rows[pl.ds(pl.multiple_of(step * STEP, STEP), STEP), :]

    def halves(pair):
        return pair[:ITEM_DEV] + pair[ITEM_DEV:]

    start = jnp.zeros((2 * ITEM_DEV, rows.shape[1]), jnp.float32)

    def rhs_step(step, acc):
        scaled = jnp.where(along(item_s, step) == own, 1.0 + along(weight_s, step), 0.0)
        return acc + jnp.dot(two_parts(scaled), held(step), preferred_element_type=jnp.float32)

    rhs = halves(lax.fori_loop(0, steps, rhs_step, start))

    def image_of(direction):
        parts = two_parts(direction)

        def step_of(step, acc):
            here = held(step)
            dots = lax.dot_general(parts, here, (((1,), (1,)), ((), ())), preferred_element_type=jnp.float32)
            scaled = jnp.where(along(item_s, step) == own, halves(dots) * along(weight_s, step), 0.0)
            return acc + jnp.dot(two_parts(scaled), here, preferred_element_type=jnp.float32)

        local = halves(lax.fori_loop(0, steps, step_of, start))
        return local + jnp.dot(direction, gram[...], precision=lax.Precision.HIGHEST) + REG * direction

    def iterate(_, state):
        solution, resid, direction, norm_now = state
        image = image_of(direction)
        alpha = norm_now / (jnp.sum(direction * image, axis=1, keepdims=True) + EPS)
        solution = solution + alpha * direction
        resid = resid - alpha * image
        norm_next = jnp.sum(resid * resid, axis=1, keepdims=True)
        direction = resid + (norm_next / (norm_now + EPS)) * direction
        return (solution, resid, direction, norm_next)

    state = (jnp.zeros_like(rhs), rhs, rhs, jnp.sum(rhs * rhs, axis=1, keepdims=True))
    solution, resid, _, _ = lax.fori_loop(0, ITERS, iterate, state)
    solution_ref[...] = solution
    resid_ref[...] = resid


def solve_kernel(
    tile, first_ref, last_ref, lo_ref, keys_ref, weight_ref, table_ref, solution_ref, resid_ref, rows, item_s, weight_s, gram, total, count
):
    block = pl.program_id(0)

    @pl.when(block == 0)
    def _():
        count[0] = 0
        gram[...] = jnp.zeros_like(gram)

    lo = lo_ref[0]
    hi = lo + table_ref.shape[0] * ITEM_DEV
    gram[...] += lax.dot_general(
        table_ref[...], table_ref[...], (((0,), (0,)), ((), ())), preferred_element_type=jnp.float32
    )
    pick_rows(block, lo, hi, tile, first_ref, last_ref, keys_ref, weight_ref, table_ref, rows, item_s, weight_s, count, total)

    @pl.when(block == pl.num_programs(0) - 1)
    def _():
        solve_items(rows, item_s, weight_s, count, gram, solution_ref, resid_ref)


def gathered_body(user_factors, tile_users, tile_items, tile_weight, live_count):
    shard = user_factors[0]
    blocks = lax.axis_size("ublk")
    tile, rank = shard.shape
    block_users = tile * lax.axis_size("salt")
    slots = tile_users.shape[2]
    groups = slots // LANES
    live = jnp.arange(slots, dtype=jnp.int32) < live_count[0, 0]
    items = tile_items[0, 0]
    key = ((items // ITEM_DEV) * block_users + tile_users[0, 0]) * ITEM_DEV + items % ITEM_DEV
    key = jnp.where(live, key, blocks * block_users * ITEM_DEV)
    key, weight = lax.sort((key, tile_weight[0, 0]), num_keys=1, is_stable=False)
    meta = lax.all_gather(jnp.stack([key.astype(jnp.float32), weight]), "ublk", axis=0)
    keys = meta[:, 0].astype(jnp.int32).reshape(blocks, groups, LANES)
    weights = meta[:, 1].reshape(blocks, groups, LANES)
    lo = (lax.axis_index("ublk") * (block_users * ITEM_DEV)).astype(jnp.int32).reshape(1)
    table = lax.all_gather(shard, ("ublk", "salt"), axis=0, tiled=True)
    smem = pl.BlockSpec(memory_space=pltpu.SMEM)
    out = jax.ShapeDtypeStruct((ITEM_DEV, rank), jnp.float32)
    whole = pl.BlockSpec((ITEM_DEV, rank), lambda b: (0, 0))
    capacity = blocks * slots + STEP
    solution, resid = pl.pallas_call(
        functools.partial(solve_kernel, tile),
        grid=(blocks,),
        in_specs=[
            smem,
            smem,
            smem,
            pl.BlockSpec((1, groups, LANES), lambda b: (b, 0, 0)),
            pl.BlockSpec((1, groups, LANES), lambda b: (b, 0, 0)),
            pl.BlockSpec((block_users, rank), lambda b: (b, 0)),
        ],
        out_specs=(whole, whole),
        out_shape=(out, out),
        scratch_shapes=[
            pltpu.VMEM((capacity, rank), jnp.bfloat16),
            pltpu.VMEM((capacity // LANES, LANES), jnp.int32),
            pltpu.VMEM((capacity // LANES, LANES), jnp.float32),
            pltpu.VMEM((rank, rank), jnp.float32),
            pltpu.VMEM((LANES, rank), jnp.float32),
            pltpu.SMEM((1,), jnp.int32),
        ],
        compiler_params=pltpu.CompilerParams(vmem_limit_bytes=40 << 20),
    )(keys[:, :, 0], keys[:, :, LANES - 1], lo, keys, weights, table)
    return (solution[None], resid[None])


def solution(mesh):
    def body(user_factors, *tiles):
        table_bytes = user_factors.size * mesh.size * user_factors.dtype.itemsize
        chosen = gathered_body if table_bytes <= TABLE_BYTES else reduced_body
        return chosen(user_factors, *tiles)

    return jax.shard_map(
        body,
        mesh=mesh,
        in_specs=(
            P("ublk", "salt", None),
            P("ublk", "salt", None),
            P("ublk", "salt", None),
            P("ublk", "salt", None),
            P("ublk", "salt"),
        ),
        out_specs=(P("salt", "ublk", None), P("salt", "ublk", None)),
        check_vma=False,
    )
```

```python
import jax
import jax.numpy as jnp
from jax import lax
from jax.experimental import pallas as pl
from jax.experimental.pallas import tpu as pltpu
from jax.sharding import PartitionSpec as P

ITERS = 8
ITEM_DEV = 32

REG = 1.0
EPS = 1e-06

LANES = 128
STEP = 2048
UNROLL = 64
TABLE_BYTES = 1 << 25


def conjugate(rhs, image_of):
    solution = jnp.zeros_like(rhs)
    resid = rhs
    direction = rhs
    norm_now = jnp.sum(resid * resid, axis=1)
    for step in range(ITERS):
        image = image_of(direction)
        alpha = norm_now / (jnp.sum(direction * image, axis=1) + EPS)
        solution = solution + alpha[:, None] * direction
        resid = resid - alpha[:, None] * image
        norm_next = jnp.sum(resid * resid, axis=1)
        direction = resid + (norm_next / (norm_now + EPS))[:, None] * direction
        norm_now = norm_next
    return (solution, resid)


def reduced_body(user_factors, tile_users, tile_items, tile_weight, live_count):
    shard = user_factors[0]
    block = lax.all_gather(shard, "salt", axis=0, tiled=True)
    contract = (((0,), (0,)), ((), ()))
    own_gram = lax.dot_general(block, block, contract, preferred_element_type=jnp.float32)
    gram = lax.psum(own_gram, "ublk")
    users = tile_users[0, 0]
    items = tile_items[0, 0]
    raw = tile_weight[0, 0]
    live = jnp.arange(users.shape[0], dtype=jnp.int32) < live_count[0, 0]
    weight = jnp.where(live, raw, jnp.zeros_like(raw))
    confid = jnp.where(live, 1.0 + raw, jnp.zeros_like(raw))
    rows = jnp.take(block, users, axis=0).astype(jnp.float32)
    column_items = ITEM_DEV * lax.axis_size("ublk")
    rhs_terms = jax.ops.segment_sum(confid[:, None] * rows, items, num_segments=column_items)

    def local_terms(whole_dir):
        along = jnp.sum(rows * whole_dir[items], axis=1) * weight
        return jax.ops.segment_sum(along[:, None] * rows, items, num_segments=column_items)

    def finish(summed, direction):
        return summed + jnp.dot(direction, gram, precision=lax.Precision.HIGHEST) + REG * direction

    rhs = lax.psum(rhs_terms, "ublk")

    def image_every(direction):
        summed = lax.psum(local_terms(direction), "ublk")
        return finish(summed, direction)

    solution_all, resid_all = conjugate(rhs, image_every)
    start = lax.axis_index("ublk") * ITEM_DEV
    solution = lax.dynamic_slice_in_dim(solution_all, start, ITEM_DEV, 0)
    resid = lax.dynamic_slice_in_dim(resid_all, start, ITEM_DEV, 0)
    return (solution[None], resid[None])


def two_parts(value):
    high = value.astype(jnp.bfloat16)
    low = (value - high.astype(jnp.float32)).astype(jnp.bfloat16)
    return jnp.concatenate([high, low], axis=0)


def pick_rows(block, lo, hi, bounds_ref, users_ref, keys_ref, weight_ref, wide, rows, item_s, weight_s, count):
    shift = ITEM_DEV.bit_length() - 1

    def group(j, at):
        key = keys_ref[0, pl.ds(j, 1), :]
        mine = (key >= lo) & (key < hi)
        item_s[pl.ds(at, 1), :] = jnp.where(mine, key & (ITEM_DEV - 1), -1)
        weight_s[pl.ds(at, 1), :] = jnp.where(mine, weight_ref[0, pl.ds(j, 1), :], 0.0)

        def some(i, carry):
            base = pl.multiple_of(i * UNROLL, UNROLL)
            taken = [wide[pl.ds(users_ref[0, 0, j * LANES + base + k], 1), :] for k in range(UNROLL)]
            rows[pl.ds(pl.multiple_of(at * LANES + base, UNROLL), UNROLL), :] = jnp.concatenate(taken, axis=0).astype(rows.dtype)
            return carry

        lax.fori_loop(0, LANES // UNROLL, some, 0)
        return at + 1

    first = bounds_ref[block, 0]
    last = bounds_ref[block, 1]
    stop = jnp.where(last > first, (last + LANES - 1) // LANES, first // LANES)
    count[0] = lax.fori_loop(first // LANES, stop, group, count[0])


def solve_items(rows, item_s, weight_s, count, gram, solution_ref, resid_ref):
    groups = STEP // LANES
    filled = count[0]
    steps = (filled + groups - 1) // groups
    for extra in range(groups - 1):
        at = filled + extra

        @pl.when(at < steps * groups)
        def _():
            rows[pl.ds(pl.multiple_of(at * LANES, LANES), LANES), :] = jnp.zeros((LANES, rows.shape[1]), rows.dtype)
            item_s[pl.ds(at, 1), :] = jnp.full((1, LANES), -1, jnp.int32)
            weight_s[pl.ds(at, 1), :] = jnp.zeros((1, LANES), jnp.float32)

    own = lax.broadcasted_iota(jnp.int32, (ITEM_DEV, STEP), 0)

    def along(ref, step):
        return jnp.concatenate([ref[pl.ds(step * groups + g, 1), :] for g in range(groups)], axis=1)

    def held(step):
        return rows[pl.ds(pl.multiple_of(step * STEP, STEP), STEP), :]

    def halves(pair):
        return pair[:ITEM_DEV] + pair[ITEM_DEV:]

    start = jnp.zeros((2 * ITEM_DEV, rows.shape[1]), jnp.float32)

    def rhs_step(step, acc):
        scaled = jnp.where(along(item_s, step) == own, 1.0 + along(weight_s, step), 0.0)
        return acc + jnp.dot(two_parts(scaled), held(step), preferred_element_type=jnp.float32)

    rhs = halves(lax.fori_loop(0, steps, rhs_step, start))

    def image_of(direction):
        parts = two_parts(direction)

        def step_of(step, acc):
            here = held(step)
            dots = lax.dot_general(parts, here, (((1,), (1,)), ((), ())), preferred_element_type=jnp.float32)
            scaled = jnp.where(along(item_s, step) == own, halves(dots) * along(weight_s, step), 0.0)
            return acc + jnp.dot(two_parts(scaled), here, preferred_element_type=jnp.float32)

        local = halves(lax.fori_loop(0, steps, step_of, start))
        return local + jnp.dot(direction, gram[...], precision=lax.Precision.HIGHEST) + REG * direction

    def iterate(_, state):
        solution, resid, direction, norm_now = state
        image = image_of(direction)
        alpha = norm_now / (jnp.sum(direction * image, axis=1, keepdims=True) + EPS)
        solution = solution + alpha * direction
        resid = resid - alpha * image
        norm_next = jnp.sum(resid * resid, axis=1, keepdims=True)
        direction = resid + (norm_next / (norm_now + EPS)) * direction
        return (solution, resid, direction, norm_next)

    state = (jnp.zeros_like(rhs), rhs, rhs, jnp.sum(rhs * rhs, axis=1, keepdims=True))
    solution, resid, _, _ = lax.fori_loop(0, ITERS, iterate, state)
    solution_ref[...] = solution
    resid_ref[...] = resid


def solve_kernel(
    bounds_ref, lo_ref, users_ref, keys_ref, weight_ref, table_ref, solution_ref, resid_ref, wide, rows, item_s, weight_s, gram, count
):
    block = pl.program_id(0)

    @pl.when(block == 0)
    def _():
        count[0] = 0
        gram[...] = jnp.zeros_like(gram)

    lo = lo_ref[0]
    hi = lo + table_ref.shape[0] * ITEM_DEV
    gram[...] += lax.dot_general(
        table_ref[...], table_ref[...], (((0,), (0,)), ((), ())), preferred_element_type=jnp.float32
    )
    wide[...] = table_ref[...].astype(jnp.float32)
    pick_rows(block, lo, hi, bounds_ref, users_ref, keys_ref, weight_ref, wide, rows, item_s, weight_s, count)

    @pl.when(block == pl.num_programs(0) - 1)
    def _():
        solve_items(rows, item_s, weight_s, count, gram, solution_ref, resid_ref)


def gathered_body(user_factors, tile_users, tile_items, tile_weight, live_count):
    shard = user_factors[0]
    blocks = lax.axis_size("ublk")
    tile, rank = shard.shape
    block_users = tile * lax.axis_size("salt")
    slots = tile_users.shape[2]
    groups = slots // LANES
    live = jnp.arange(slots, dtype=jnp.int32) < live_count[0, 0]
    items = tile_items[0, 0]
    key = ((items // ITEM_DEV) * block_users + tile_users[0, 0]) * ITEM_DEV + items % ITEM_DEV
    key = jnp.where(live, key, blocks * block_users * ITEM_DEV)
    key, weight = lax.sort((key, tile_weight[0, 0]), num_keys=1, is_stable=False)
    meta = lax.all_gather(jnp.stack([key.astype(jnp.float32), weight]), "ublk", axis=0)
    keys = meta[:, 0].astype(jnp.int32).reshape(blocks, groups, LANES)
    weights = meta[:, 1].reshape(blocks, groups, LANES)
    lo = (lax.axis_index("ublk") * (block_users * ITEM_DEV)).astype(jnp.int32).reshape(1)
    table = lax.all_gather(shard, ("ublk", "salt"), axis=0, tiled=True)
    hi = lo + block_users * ITEM_DEV
    flat = keys.reshape(blocks, slots)
    bounds = jnp.stack([jnp.sum((flat < lo).astype(jnp.int32), axis=1), jnp.sum((flat < hi).astype(jnp.int32), axis=1)], axis=1)
    users = jnp.clip((flat - lo) // ITEM_DEV, 0, block_users - 1).reshape(blocks, 1, slots)
    smem = pl.BlockSpec(memory_space=pltpu.SMEM)
    out = jax.ShapeDtypeStruct((ITEM_DEV, rank), jnp.float32)
    whole = pl.BlockSpec((ITEM_DEV, rank), lambda b: (0, 0))
    capacity = blocks * slots + STEP
    solution, resid = pl.pallas_call(
        solve_kernel,
        grid=(blocks,),
        in_specs=[
            smem,
            smem,
            pl.BlockSpec((1, 1, slots), lambda b: (b, 0, 0), memory_space=pltpu.SMEM),
            pl.BlockSpec((1, groups, LANES), lambda b: (b, 0, 0)),
            pl.BlockSpec((1, groups, LANES), lambda b: (b, 0, 0)),
            pl.BlockSpec((block_users, rank), lambda b: (b, 0)),
        ],
        out_specs=(whole, whole),
        out_shape=(out, out),
        scratch_shapes=[
            pltpu.VMEM((block_users, rank), jnp.float32),
            pltpu.VMEM((capacity, rank), jnp.bfloat16),
            pltpu.VMEM((capacity // LANES, LANES), jnp.int32),
            pltpu.VMEM((capacity // LANES, LANES), jnp.float32),
            pltpu.VMEM((rank, rank), jnp.float32),
            pltpu.SMEM((1,), jnp.int32),
        ],
        compiler_params=pltpu.CompilerParams(vmem_limit_bytes=40 << 20),
    )(bounds, lo, users, keys, weights, table)
    return (solution[None], resid[None])


def solution(mesh):
    def body(user_factors, *tiles):
        table_bytes = user_factors.size * mesh.size * user_factors.dtype.itemsize
        chosen = gathered_body if table_bytes <= TABLE_BYTES else reduced_body
        return chosen(user_factors, *tiles)

    return jax.shard_map(
        body,
        mesh=mesh,
        in_specs=(
            P("ublk", "salt", None),
            P("ublk", "salt", None),
            P("ublk", "salt", None),
            P("ublk", "salt", None),
            P("ublk", "salt"),
        ),
        out_specs=(P("salt", "ublk", None), P("salt", "ublk", None)),
        check_vma=False,
    )
```

```python
import functools

import jax
import jax.numpy as jnp
from jax import lax
from jax.experimental import pallas as pl
from jax.experimental.pallas import tpu as pltpu
from jax.sharding import PartitionSpec as P

ITERS = 8
ITEM_DEV = 32

REG = 1.0
EPS = 1e-06

LANES = 128
STEP = 2048
UNROLL = 64
LAG = 3
TABLE_BYTES = 1 << 25


def conjugate(rhs, image_of):
    solution = jnp.zeros_like(rhs)
    resid = rhs
    direction = rhs
    norm_now = jnp.sum(resid * resid, axis=1)
    for step in range(ITERS):
        image = image_of(direction)
        alpha = norm_now / (jnp.sum(direction * image, axis=1) + EPS)
        solution = solution + alpha[:, None] * direction
        resid = resid - alpha[:, None] * image
        norm_next = jnp.sum(resid * resid, axis=1)
        direction = resid + (norm_next / (norm_now + EPS))[:, None] * direction
        norm_now = norm_next
    return (solution, resid)


def reduced_body(user_factors, tile_users, tile_items, tile_weight, live_count):
    shard = user_factors[0]
    block = lax.all_gather(shard, "salt", axis=0, tiled=True)
    contract = (((0,), (0,)), ((), ()))
    own_gram = lax.dot_general(block, block, contract, preferred_element_type=jnp.float32)
    gram = lax.psum(own_gram, "ublk")
    users = tile_users[0, 0]
    items = tile_items[0, 0]
    raw = tile_weight[0, 0]
    live = jnp.arange(users.shape[0], dtype=jnp.int32) < live_count[0, 0]
    weight = jnp.where(live, raw, jnp.zeros_like(raw))
    confid = jnp.where(live, 1.0 + raw, jnp.zeros_like(raw))
    rows = jnp.take(block, users, axis=0).astype(jnp.float32)
    column_items = ITEM_DEV * lax.axis_size("ublk")
    rhs_terms = jax.ops.segment_sum(confid[:, None] * rows, items, num_segments=column_items)

    def local_terms(whole_dir):
        along = jnp.sum(rows * whole_dir[items], axis=1) * weight
        return jax.ops.segment_sum(along[:, None] * rows, items, num_segments=column_items)

    def finish(summed, direction):
        return summed + jnp.dot(direction, gram, precision=lax.Precision.HIGHEST) + REG * direction

    rhs = lax.psum(rhs_terms, "ublk")

    def image_every(direction):
        summed = lax.psum(local_terms(direction), "ublk")
        return finish(summed, direction)

    solution_all, resid_all = conjugate(rhs, image_every)
    start = lax.axis_index("ublk") * ITEM_DEV
    solution = lax.dynamic_slice_in_dim(solution_all, start, ITEM_DEV, 0)
    resid = lax.dynamic_slice_in_dim(resid_all, start, ITEM_DEV, 0)
    return (solution[None], resid[None])


def two_parts(value):
    high = value.astype(jnp.bfloat16)
    low = (value - high.astype(jnp.float32)).astype(jnp.bfloat16)
    return jnp.concatenate([high, low], axis=0)


def pick_rows(lo, hi, first, last, users_ref, keys_ref, weight_ref, wide, rows, item_s, weight_s, count):
    def group(j, at):
        key = keys_ref[0, pl.ds(j, 1), :]
        mine = (key >= lo) & (key < hi)
        item_s[pl.ds(at, 1), :] = jnp.where(mine, key & (ITEM_DEV - 1), -1)
        weight_s[pl.ds(at, 1), :] = jnp.where(mine, weight_ref[0, pl.ds(j, 1), :], 0.0)

        def some(i, carry):
            base = pl.multiple_of(i * UNROLL, UNROLL)
            taken = [wide[pl.ds(users_ref[0, 0, j * LANES + base + k], 1), :] for k in range(UNROLL)]
            to = pl.ds(pl.multiple_of(at * LANES + base, UNROLL), UNROLL)
            rows[to, :] = jnp.concatenate(taken, axis=0).astype(rows.dtype)
            return carry

        lax.fori_loop(0, LANES // UNROLL, some, 0)
        return at + 1

    stop = jnp.where(last > first, (last + LANES - 1) // LANES, first // LANES)
    count[0] = lax.fori_loop(first // LANES, stop, group, count[0])


def absorb(base, place_ref, bounds_ref, users_ref, keys_ref, weight_ref, pieces, wide, rows, item_s, weight_s, gram, count):
    tile = pieces[0].shape[0]
    users = tile * len(pieces)
    added = None
    for away, piece in enumerate(pieces):
        here = piece[...]
        start = pl.multiple_of((place_ref[1] ^ away) * tile, tile)
        wide[pl.ds(start, tile), :] = here.astype(jnp.float32)
        term = lax.dot_general(here, here, (((0,), (0,)), ((), ())), preferred_element_type=jnp.float32)
        added = term if added is None else added + term
    gram[...] += added
    lo = place_ref[0] * (users * ITEM_DEV)
    hi = lo + users * ITEM_DEV
    pick_rows(
        lo, hi, bounds_ref[2 * base], bounds_ref[2 * base + 1], users_ref, keys_ref, weight_ref, wide, rows, item_s, weight_s, count
    )


def pieces_of(refs):
    own_near, own_far, next_near, next_far = refs
    return [own_near.at[0], next_near.at[0], own_far.at[0], next_far.at[0]]


def early_kernel(base, sets, place_ref, bounds_ref, users_ref, keys_ref, weight_ref, *refs):
    tables, (rows_out, item_s, weight_s, gram, count), (wide, rows, sems) = refs[: 4 * sets], refs[4 * sets : -3], refs[-3:]
    step = pl.program_id(0)

    @pl.when(step == 0)
    def _():
        count[0] = 0
        gram[...] = jnp.zeros_like(gram)

    for at in range(sets):

        @pl.when(step // 2 == at)
        def _(at=at):
            absorb(
                base + step, place_ref, bounds_ref, users_ref, keys_ref, weight_ref,
                pieces_of(tables[4 * at : 4 * at + 4]), wide, rows, item_s, weight_s, gram, count,
            )

    @pl.when(step == pl.num_programs(0) - 1)
    def _():
        move_groups(rows, rows_out, 0, count[0], sems)


def move_groups(source, target, to, number, sems):
    depth = sems.shape[0]

    def copy(i):
        return pltpu.make_async_copy(
            source.at[pl.ds(pl.multiple_of(i * LANES, LANES), LANES), :],
            target.at[pl.ds(pl.multiple_of((to + i) * LANES, LANES), LANES), :],
            sems.at[i % depth],
        )

    def start(i, carry):
        @pl.when(i >= depth)
        def _():
            copy(i - depth).wait()

        copy(i).start()
        return carry

    def finish(i, carry):
        copy(i).wait()
        return carry

    lax.fori_loop(0, number, start, 0)
    lax.fori_loop(jnp.maximum(number - depth, 0), number, finish, 0)


def last_kernel(base, earlier, place_ref, bounds_ref, users_ref, keys_ref, weight_ref, *refs):
    tables, before, (solution_ref, resid_ref) = refs[:4], refs[4 : 4 + 5 * earlier], refs[4 + 5 * earlier : 6 + 5 * earlier]
    wide, rows, item_s, weight_s, gram, count, sems = refs[6 + 5 * earlier :]
    step = pl.program_id(0)

    @pl.when(step == 0)
    def _():
        gram[...] = jnp.zeros_like(gram)
        total = 0
        for at in range(earlier):
            rows_ref, item_ref, weight_in, gram_ref, count_ref = before[5 * at : 5 * at + 5]
            number = count_ref[0]
            move_groups(rows_ref, rows, total, number, sems)

            def line(i, carry, item_ref=item_ref, weight_in=weight_in, total=total):
                item_s[pl.ds(total + i, 1), :] = item_ref[pl.ds(i, 1), :]
                weight_s[pl.ds(total + i, 1), :] = weight_in[pl.ds(i, 1), :]
                return carry

            lax.fori_loop(0, number, line, 0)
            gram[...] += gram_ref[...]
            total = total + number
        count[0] = total

    absorb(
        base + step, place_ref, bounds_ref, users_ref, keys_ref, weight_ref,
        pieces_of(tables), wide, rows, item_s, weight_s, gram, count,
    )

    @pl.when(step == pl.num_programs(0) - 1)
    def _():
        solve_items(rows, item_s, weight_s, count, gram, solution_ref, resid_ref)


def solve_items(rows, item_s, weight_s, count, gram, solution_ref, resid_ref):
    groups = STEP // LANES
    filled = count[0]
    steps = (filled + groups - 1) // groups
    for extra in range(groups - 1):
        at = filled + extra

        @pl.when(at < steps * groups)
        def _():
            rows[pl.ds(pl.multiple_of(at * LANES, LANES), LANES), :] = jnp.zeros((LANES, rows.shape[1]), rows.dtype)
            item_s[pl.ds(at, 1), :] = jnp.full((1, LANES), -1, jnp.int32)
            weight_s[pl.ds(at, 1), :] = jnp.zeros((1, LANES), jnp.float32)

    own = lax.broadcasted_iota(jnp.int32, (ITEM_DEV, STEP), 0)

    def along(ref, step):
        return jnp.concatenate([ref[pl.ds(step * groups + g, 1), :] for g in range(groups)], axis=1)

    def held(step):
        return rows[pl.ds(pl.multiple_of(step * STEP, STEP), STEP), :]

    def halves(pair):
        return pair[:ITEM_DEV] + pair[ITEM_DEV:]

    start = jnp.zeros((2 * ITEM_DEV, rows.shape[1]), jnp.float32)

    def rhs_step(step, acc):
        scaled = jnp.where(along(item_s, step) == own, 1.0 + along(weight_s, step), 0.0)
        return acc + jnp.dot(two_parts(scaled), held(step), preferred_element_type=jnp.float32)

    rhs = halves(lax.fori_loop(0, steps, rhs_step, start))

    def image_of(direction):
        parts = two_parts(direction)

        def step_of(step, acc):
            here = held(step)
            dots = lax.dot_general(parts, here, (((1,), (1,)), ((), ())), preferred_element_type=jnp.float32)
            scaled = jnp.where(along(item_s, step) == own, halves(dots) * along(weight_s, step), 0.0)
            return acc + jnp.dot(two_parts(scaled), here, preferred_element_type=jnp.float32)

        local = halves(lax.fori_loop(0, steps, step_of, start))
        return local + jnp.dot(direction, gram[...], precision=lax.Precision.HIGHEST) + REG * direction

    def iterate(_, state):
        solution, resid, direction, norm_now = state
        image = image_of(direction)
        alpha = norm_now / (jnp.sum(direction * image, axis=1, keepdims=True) + EPS)
        solution = solution + alpha * direction
        resid = resid - alpha * image
        norm_next = jnp.sum(resid * resid, axis=1, keepdims=True)
        direction = resid + (norm_next / (norm_now + EPS)) * direction
        return (solution, resid, direction, norm_next)

    state = (jnp.zeros_like(rhs), rhs, rhs, jnp.sum(rhs * rhs, axis=1, keepdims=True))
    solution, resid, _, _ = lax.fori_loop(0, ITERS, iterate, state)
    solution_ref[...] = solution
    resid_ref[...] = resid


def exchange(value, axis, away):
    return lax.ppermute(value, axis, [(i, i ^ away) for i in range(lax.axis_size(axis))])


def tie(value, *others):
    return lax.optimization_barrier((value, *others))[0]


def gathered_body(user_factors, tile_users, tile_items, tile_weight, live_count):
    shard = user_factors[0]
    blocks = lax.axis_size("ublk")
    salts = lax.axis_size("salt")
    tile, rank = shard.shape
    block_users = tile * salts
    slots = tile_users.shape[2]
    lines = slots // LANES
    live = jnp.arange(slots, dtype=jnp.int32) < live_count[0, 0]
    items = tile_items[0, 0]
    key = ((items // ITEM_DEV) * block_users + tile_users[0, 0]) * ITEM_DEV + items % ITEM_DEV
    key = jnp.where(live, key, blocks * block_users * ITEM_DEV)
    key, weight = lax.sort((key, tile_weight[0, 0]), num_keys=1, is_stable=False)
    meta = jnp.stack([key.astype(jnp.float32), weight])[None]
    away = 1
    while away < blocks:
        meta = jnp.concatenate([meta, exchange(meta, "ublk", away)])
        away *= 2
    keys = meta[:, 0].astype(jnp.int32)
    weights = meta[:, 1].reshape(blocks, lines, LANES)
    me = lax.axis_index("ublk").astype(jnp.int32)
    lo = me * (block_users * ITEM_DEV)
    hi = lo + block_users * ITEM_DEV
    bounds = jnp.stack([jnp.sum((keys < lo).astype(jnp.int32), axis=1), jnp.sum((keys < hi).astype(jnp.int32), axis=1)], axis=1)
    users = jnp.clip((keys - lo) // ITEM_DEV, 0, block_users - 1).reshape(blocks, 1, slots)
    place = jnp.stack([me, lax.axis_index("salt").astype(jnp.int32)])
    data = (place, bounds.reshape(-1), users, keys.reshape(blocks, lines, LANES), weights)

    half = tile // 2
    near = []
    own = []

    def specs(base, sets):
        def block_at(i, place_ref, _):
            return (base + i, 0, 0)

        tables = []
        for at in range(sets):
            for _ in range(2):
                for row in range(2):
                    tables.append(
                        pl.BlockSpec((1, tile, rank), lambda i, p, q, at=at, row=row: (2 * row + jnp.clip(i - 2 * at, 0, 1), 0, 0))
                    )
        return [
            pl.BlockSpec((1, 1, slots), block_at, memory_space=pltpu.SMEM),
            pl.BlockSpec((1, lines, LANES), block_at),
            pl.BlockSpec((1, lines, LANES), block_at),
            *tables,
        ]

    def tables_of(start, stop):
        return [part for at in range(start, stop) for part in (own[at], own[at], near[at], near[at])]

    def early(start, stop):
        sets = stop - start
        capacity = 2 * sets * slots
        fixed = lambda i, p, q: (0, 0)
        return pl.pallas_call(
            functools.partial(early_kernel, 2 * start, sets),
            grid_spec=pltpu.PrefetchScalarGridSpec(
                num_scalar_prefetch=2,
                grid=(2 * sets,),
                in_specs=specs(2 * start, sets),
                out_specs=[
                    pl.BlockSpec(memory_space=pl.ANY),
                    pl.BlockSpec((capacity // LANES, LANES), fixed),
                    pl.BlockSpec((capacity // LANES, LANES), fixed),
                    pl.BlockSpec((rank, rank), fixed),
                    pl.BlockSpec(memory_space=pltpu.SMEM),
                ],
                scratch_shapes=[
                    pltpu.VMEM((block_users, rank), jnp.float32),
                    pltpu.VMEM((capacity, rank), jnp.bfloat16),
                    pltpu.SemaphoreType.DMA((8,)),
                ],
            ),
            out_shape=[
                jax.ShapeDtypeStruct((capacity, rank), jnp.bfloat16),
                jax.ShapeDtypeStruct((capacity // LANES, LANES), jnp.int32),
                jax.ShapeDtypeStruct((capacity // LANES, LANES), jnp.float32),
                jax.ShapeDtypeStruct((rank, rank), jnp.float32),
                jax.ShapeDtypeStruct((1,), jnp.int32),
            ],
            compiler_params=pltpu.CompilerParams(vmem_limit_bytes=20 << 20),
            cost_estimate=pl.CostEstimate(flops=sets << 32, bytes_accessed=sets << 23, transcendentals=0),
        )(*data, *tables_of(start, stop))

    far = [shard]
    for away in range(2, blocks, 2):
        far.append(exchange(tie(shard, far[-1]), "ublk", away))
    sets = len(far)
    states = []
    for at, part in enumerate(far):
        if at > 0:
            part = tie(part, beside, above)
        beside = exchange(part, "ublk", 1)
        above = exchange(part, "salt", 2)
        if at >= LAG:
            states.append(early(at - LAG, at - LAG + 1))
            beside = tie(beside, states[-1][4])
            above = tie(above, states[-1][4])
        over = exchange(beside[:half], "salt", 2)
        under = exchange(above[half:], "ublk", 1)
        if at < sets - 1:
            mine = jnp.concatenate([part, beside, above, over, under])
            own.append(mine.reshape(salts, tile, rank))
            near.append(exchange(mine, "salt", 1).reshape(salts, tile, rank))
        else:
            most = jnp.concatenate([part, beside, above])
            rest = jnp.concatenate([over, under])
            own.append(jnp.concatenate([most, rest]).reshape(salts, tile, rank))
            near.append(jnp.concatenate([exchange(most, "salt", 1), exchange(rest, "salt", 1)]).reshape(salts, tile, rank))
    for at in range(len(states), sets - 1):
        states.append(early(at, at + 1))

    capacity = blocks * slots + STEP
    out = jax.ShapeDtypeStruct((ITEM_DEV, rank), jnp.float32)
    whole = pl.BlockSpec((ITEM_DEV, rank), lambda i, p, q: (0, 0))
    before_specs = []
    for state in states:
        before_specs += [
            pl.BlockSpec(memory_space=pl.ANY),
            pl.BlockSpec(state[1].shape, lambda i, p, q: (0, 0)),
            pl.BlockSpec(state[2].shape, lambda i, p, q: (0, 0)),
            pl.BlockSpec(state[3].shape, lambda i, p, q: (0, 0)),
            pl.BlockSpec(memory_space=pltpu.SMEM),
        ]
    solution, resid = pl.pallas_call(
        functools.partial(last_kernel, 2 * (sets - 1), len(states)),
        grid_spec=pltpu.PrefetchScalarGridSpec(
            num_scalar_prefetch=2,
            grid=(2,),
            in_specs=specs(2 * (sets - 1), 1) + before_specs,
            out_specs=[whole, whole],
            scratch_shapes=[
                pltpu.VMEM((block_users, rank), jnp.float32),
                pltpu.VMEM((capacity, rank), jnp.bfloat16),
                pltpu.VMEM((capacity // LANES, LANES), jnp.int32),
                pltpu.VMEM((capacity // LANES, LANES), jnp.float32),
                pltpu.VMEM((rank, rank), jnp.float32),
                pltpu.SMEM((1,), jnp.int32),
                pltpu.SemaphoreType.DMA((8,)),
            ],
        ),
        out_shape=[out, out],
        compiler_params=pltpu.CompilerParams(vmem_limit_bytes=32 << 20),
    )(*data, *tables_of(sets - 1, sets), *[part for state in states for part in state])
    return (solution[None], resid[None])


def solution(mesh):
    def body(user_factors, *tiles):
        table_bytes = user_factors.size * mesh.size * user_factors.dtype.itemsize
        blocks = mesh.shape["ublk"]
        swaps = mesh.shape["salt"] == 4 and blocks >= 8 and blocks & (blocks - 1) == 0
        chosen = gathered_body if swaps and table_bytes <= TABLE_BYTES else reduced_body
        return chosen(user_factors, *tiles)

    return jax.shard_map(
        body,
        mesh=mesh,
        in_specs=(
            P("ublk", "salt", None),
            P("ublk", "salt", None),
            P("ublk", "salt", None),
            P("ublk", "salt", None),
            P("ublk", "salt"),
        ),
        out_specs=(P("salt", "ublk", None), P("salt", "ublk", None)),
        check_vma=False,
    )
```

```python
import functools

import jax
import jax.numpy as jnp
from jax import lax
from jax.experimental import pallas as pl
from jax.experimental.pallas import tpu as pltpu
from jax.sharding import PartitionSpec as P

ITERS = 8
ITEM_DEV = 32

REG = 1.0
EPS = 1e-06

LANES = 128
STEP = 2048
UNROLL = 64
LAG = 3
TABLE_BYTES = 1 << 25


def conjugate(rhs, image_of):
    solution = jnp.zeros_like(rhs)
    resid = rhs
    direction = rhs
    norm_now = jnp.sum(resid * resid, axis=1)
    for step in range(ITERS):
        image = image_of(direction)
        alpha = norm_now / (jnp.sum(direction * image, axis=1) + EPS)
        solution = solution + alpha[:, None] * direction
        resid = resid - alpha[:, None] * image
        norm_next = jnp.sum(resid * resid, axis=1)
        direction = resid + (norm_next / (norm_now + EPS))[:, None] * direction
        norm_now = norm_next
    return (solution, resid)


def reduced_body(user_factors, tile_users, tile_items, tile_weight, live_count):
    shard = user_factors[0]
    block = lax.all_gather(shard, "salt", axis=0, tiled=True)
    contract = (((0,), (0,)), ((), ()))
    own_gram = lax.dot_general(block, block, contract, preferred_element_type=jnp.float32)
    gram = lax.psum(own_gram, "ublk")
    users = tile_users[0, 0]
    items = tile_items[0, 0]
    raw = tile_weight[0, 0]
    live = jnp.arange(users.shape[0], dtype=jnp.int32) < live_count[0, 0]
    weight = jnp.where(live, raw, jnp.zeros_like(raw))
    confid = jnp.where(live, 1.0 + raw, jnp.zeros_like(raw))
    rows = jnp.take(block, users, axis=0).astype(jnp.float32)
    column_items = ITEM_DEV * lax.axis_size("ublk")
    rhs_terms = jax.ops.segment_sum(confid[:, None] * rows, items, num_segments=column_items)

    def local_terms(whole_dir):
        along = jnp.sum(rows * whole_dir[items], axis=1) * weight
        return jax.ops.segment_sum(along[:, None] * rows, items, num_segments=column_items)

    def finish(summed, direction):
        return summed + jnp.dot(direction, gram, precision=lax.Precision.HIGHEST) + REG * direction

    rhs = lax.psum(rhs_terms, "ublk")

    def image_every(direction):
        summed = lax.psum(local_terms(direction), "ublk")
        return finish(summed, direction)

    solution_all, resid_all = conjugate(rhs, image_every)
    start = lax.axis_index("ublk") * ITEM_DEV
    solution = lax.dynamic_slice_in_dim(solution_all, start, ITEM_DEV, 0)
    resid = lax.dynamic_slice_in_dim(resid_all, start, ITEM_DEV, 0)
    return (solution[None], resid[None])


def two_parts(value):
    high = value.astype(jnp.bfloat16)
    low = (value - high.astype(jnp.float32)).astype(jnp.bfloat16)
    return jnp.concatenate([high, low], axis=0)


def pick_rows(lo, hi, first, last, users_ref, keys_ref, weight_ref, wide, rows, item_s, weight_s, count):
    def group(j, at):
        key = keys_ref[0, pl.ds(j, 1), :]
        mine = (key >= lo) & (key < hi)
        item_s[pl.ds(at, 1), :] = jnp.where(mine, key & (ITEM_DEV - 1), -1)
        weight_s[pl.ds(at, 1), :] = jnp.where(mine, weight_ref[0, pl.ds(j, 1), :], 0.0)

        def some(i, carry):
            base = pl.multiple_of(i * UNROLL, UNROLL)
            taken = [wide[pl.ds(users_ref[0, 0, j * LANES + base + k], 1), :] for k in range(UNROLL)]
            to = pl.ds(pl.multiple_of(at * LANES + base, UNROLL), UNROLL)
            rows[to, :] = jnp.concatenate(taken, axis=0).astype(rows.dtype)
            return carry

        lax.fori_loop(0, LANES // UNROLL, some, 0)
        return at + 1

    stop = jnp.where(last > first, (last + LANES - 1) // LANES, first // LANES)
    count[0] = lax.fori_loop(first // LANES, stop, group, count[0])


def absorb(base, place_ref, bounds_ref, users_ref, keys_ref, weight_ref, pieces, wide, rows, item_s, weight_s, gram, count):
    tile = pieces[0].shape[0]
    users = tile * len(pieces)
    added = None
    for away, piece in enumerate(pieces):
        here = piece[...]
        start = pl.multiple_of((place_ref[1] ^ away) * tile, tile)
        wide[pl.ds(start, tile), :] = here.astype(jnp.float32)
        term = lax.dot_general(here, here, (((0,), (0,)), ((), ())), preferred_element_type=jnp.float32)
        added = term if added is None else added + term
    gram[...] += added
    lo = place_ref[0] * (users * ITEM_DEV)
    hi = lo + users * ITEM_DEV
    pick_rows(
        lo, hi, bounds_ref[2 * base], bounds_ref[2 * base + 1], users_ref, keys_ref, weight_ref, wide, rows, item_s, weight_s, count
    )


def pieces_of(refs):
    own_near, own_far, next_near, next_far = refs
    return [own_near.at[0], next_near.at[0], own_far.at[0], next_far.at[0]]


def early_kernel(base, sets, place_ref, bounds_ref, users_ref, keys_ref, weight_ref, *refs):
    tables, (rows_out, item_s, weight_s, gram, count), (wide, rows, sems) = refs[: 4 * sets], refs[4 * sets : -3], refs[-3:]
    step = pl.program_id(0)

    @pl.when(step == 0)
    def _():
        count[0] = 0
        gram[...] = jnp.zeros_like(gram)

    for at in range(sets):

        @pl.when(step // 2 == at)
        def _(at=at):
            absorb(
                base + step, place_ref, bounds_ref, users_ref, keys_ref, weight_ref,
                pieces_of(tables[4 * at : 4 * at + 4]), wide, rows, item_s, weight_s, gram, count,
            )

    @pl.when(step == pl.num_programs(0) - 1)
    def _():
        move_groups(rows, rows_out, 0, count[0], sems)


def move_groups(source, target, to, number, sems):
    depth = sems.shape[0]

    def copy(i):
        return pltpu.make_async_copy(
            source.at[pl.ds(pl.multiple_of(i * LANES, LANES), LANES), :],
            target.at[pl.ds(pl.multiple_of((to + i) * LANES, LANES), LANES), :],
            sems.at[i % depth],
        )

    def start(i, carry):
        @pl.when(i >= depth)
        def _():
            copy(i - depth).wait()

        copy(i).start()
        return carry

    def finish(i, carry):
        copy(i).wait()
        return carry

    lax.fori_loop(0, number, start, 0)
    lax.fori_loop(jnp.maximum(number - depth, 0), number, finish, 0)


def last_kernel(base, earlier, place_ref, bounds_ref, users_ref, keys_ref, weight_ref, *refs):
    tables, before, (solution_ref, resid_ref) = refs[:4], refs[4 : 4 + 5 * earlier], refs[4 + 5 * earlier : 6 + 5 * earlier]
    wide, rows, item_s, weight_s, gram, count, sems = refs[6 + 5 * earlier :]
    step = pl.program_id(0)

    @pl.when(step == 0)
    def _():
        gram[...] = jnp.zeros_like(gram)
        total = 0
        for at in range(earlier):
            rows_ref, item_ref, weight_in, gram_ref, count_ref = before[5 * at : 5 * at + 5]
            number = count_ref[0]
            move_groups(rows_ref, rows, total, number, sems)

            def line(i, carry, item_ref=item_ref, weight_in=weight_in, total=total):
                item_s[pl.ds(total + i, 1), :] = item_ref[pl.ds(i, 1), :]
                weight_s[pl.ds(total + i, 1), :] = weight_in[pl.ds(i, 1), :]
                return carry

            lax.fori_loop(0, number, line, 0)
            gram[...] += gram_ref[...]
            total = total + number
        count[0] = total

    absorb(
        base + step, place_ref, bounds_ref, users_ref, keys_ref, weight_ref,
        pieces_of(tables), wide, rows, item_s, weight_s, gram, count,
    )

    @pl.when(step == pl.num_programs(0) - 1)
    def _():
        solve_items(rows, item_s, weight_s, count, gram, solution_ref, resid_ref)


def solve_items(rows, item_s, weight_s, count, gram, solution_ref, resid_ref):
    groups = STEP // LANES
    filled = count[0]
    steps = (filled + groups - 1) // groups
    for extra in range(groups - 1):
        at = filled + extra

        @pl.when(at < steps * groups)
        def _():
            rows[pl.ds(pl.multiple_of(at * LANES, LANES), LANES), :] = jnp.zeros((LANES, rows.shape[1]), rows.dtype)
            item_s[pl.ds(at, 1), :] = jnp.full((1, LANES), -1, jnp.int32)
            weight_s[pl.ds(at, 1), :] = jnp.zeros((1, LANES), jnp.float32)

    own = lax.broadcasted_iota(jnp.int32, (ITEM_DEV, STEP), 0)

    def along(ref, step):
        return jnp.concatenate([ref[pl.ds(step * groups + g, 1), :] for g in range(groups)], axis=1)

    def held(step):
        return rows[pl.ds(pl.multiple_of(step * STEP, STEP), STEP), :]

    def halves(pair):
        return pair[:ITEM_DEV] + pair[ITEM_DEV:]

    start = jnp.zeros((2 * ITEM_DEV, rows.shape[1]), jnp.float32)

    def rhs_step(step, acc):
        scaled = jnp.where(along(item_s, step) == own, 1.0 + along(weight_s, step), 0.0)
        return acc + jnp.dot(two_parts(scaled), held(step), preferred_element_type=jnp.float32)

    rhs = halves(lax.fori_loop(0, steps, rhs_step, start))

    def image_of(direction):
        parts = two_parts(direction)

        def step_of(step, acc):
            here = held(step)
            dots = lax.dot_general(parts, here, (((1,), (1,)), ((), ())), preferred_element_type=jnp.float32)
            scaled = jnp.where(along(item_s, step) == own, halves(dots) * along(weight_s, step), 0.0)
            return acc + jnp.dot(two_parts(scaled), here, preferred_element_type=jnp.float32)

        local = halves(lax.fori_loop(0, steps, step_of, start))
        return local + jnp.dot(direction, gram[...], precision=lax.Precision.HIGHEST) + REG * direction

    def iterate(_, state):
        solution, resid, direction, norm_now = state
        image = image_of(direction)
        alpha = norm_now / (jnp.sum(direction * image, axis=1, keepdims=True) + EPS)
        solution = solution + alpha * direction
        resid = resid - alpha * image
        norm_next = jnp.sum(resid * resid, axis=1, keepdims=True)
        direction = resid + (norm_next / (norm_now + EPS)) * direction
        return (solution, resid, direction, norm_next)

    state = (jnp.zeros_like(rhs), rhs, rhs, jnp.sum(rhs * rhs, axis=1, keepdims=True))
    solution, resid, _, _ = lax.fori_loop(0, ITERS, iterate, state)
    solution_ref[...] = solution
    resid_ref[...] = resid


def exchange(value, axis, away):
    return lax.ppermute(value, axis, [(i, i ^ away) for i in range(lax.axis_size(axis))])


def tie(value, *others):
    return lax.optimization_barrier((value, *others))[0]


def gathered_body(user_factors, tile_users, tile_items, tile_weight, live_count):
    shard = user_factors[0]
    blocks = lax.axis_size("ublk")
    salts = lax.axis_size("salt")
    tile, rank = shard.shape
    block_users = tile * salts
    slots = tile_users.shape[2]
    lines = slots // LANES
    live = jnp.arange(slots, dtype=jnp.int32) < live_count[0, 0]
    items = tile_items[0, 0]
    key = ((items // ITEM_DEV) * block_users + tile_users[0, 0]) * ITEM_DEV + items % ITEM_DEV
    key = jnp.where(live, key, blocks * block_users * ITEM_DEV)
    key, weight = lax.sort((key, tile_weight[0, 0]), num_keys=1, is_stable=False)
    meta = jnp.stack([key.astype(jnp.float32), weight])[None]
    meta = jnp.concatenate([meta, exchange(meta, "ublk", 1)])
    meta = jnp.concatenate([meta] + [exchange(meta, "ublk", away) for away in range(2, blocks, 2)])
    keys = meta[:, 0].astype(jnp.int32)
    weights = meta[:, 1].reshape(blocks, lines, LANES)
    me = lax.axis_index("ublk").astype(jnp.int32)
    lo = me * (block_users * ITEM_DEV)
    hi = lo + block_users * ITEM_DEV
    bounds = jnp.stack([jnp.sum((keys < lo).astype(jnp.int32), axis=1), jnp.sum((keys < hi).astype(jnp.int32), axis=1)], axis=1)
    users = jnp.clip((keys - lo) // ITEM_DEV, 0, block_users - 1).reshape(blocks, 1, slots)
    place = jnp.stack([me, lax.axis_index("salt").astype(jnp.int32)])
    data = (place, bounds.reshape(-1), users, keys.reshape(blocks, lines, LANES), weights)

    half = tile // 2
    near = []
    own = []

    def specs(base, sets):
        def block_at(i, place_ref, _):
            return (base + i, 0, 0)

        tables = []
        for at in range(sets):
            for _ in range(2):
                for row in range(2):
                    tables.append(
                        pl.BlockSpec((1, tile, rank), lambda i, p, q, at=at, row=row: (2 * row + jnp.clip(i - 2 * at, 0, 1), 0, 0))
                    )
        return [
            pl.BlockSpec((1, 1, slots), block_at, memory_space=pltpu.SMEM),
            pl.BlockSpec((1, lines, LANES), block_at),
            pl.BlockSpec((1, lines, LANES), block_at),
            *tables,
        ]

    def tables_of(start, stop):
        return [part for at in range(start, stop) for part in (own[at], own[at], near[at], near[at])]

    def early(start, stop):
        sets = stop - start
        capacity = 2 * sets * slots
        fixed = lambda i, p, q: (0, 0)
        return pl.pallas_call(
            functools.partial(early_kernel, 2 * start, sets),
            grid_spec=pltpu.PrefetchScalarGridSpec(
                num_scalar_prefetch=2,
                grid=(2 * sets,),
                in_specs=specs(2 * start, sets),
                out_specs=[
                    pl.BlockSpec(memory_space=pl.ANY),
                    pl.BlockSpec((capacity // LANES, LANES), fixed),
                    pl.BlockSpec((capacity // LANES, LANES), fixed),
                    pl.BlockSpec((rank, rank), fixed),
                    pl.BlockSpec(memory_space=pltpu.SMEM),
                ],
                scratch_shapes=[
                    pltpu.VMEM((block_users, rank), jnp.float32),
                    pltpu.VMEM((capacity, rank), jnp.bfloat16),
                    pltpu.SemaphoreType.DMA((8,)),
                ],
            ),
            out_shape=[
                jax.ShapeDtypeStruct((capacity, rank), jnp.bfloat16),
                jax.ShapeDtypeStruct((capacity // LANES, LANES), jnp.int32),
                jax.ShapeDtypeStruct((capacity // LANES, LANES), jnp.float32),
                jax.ShapeDtypeStruct((rank, rank), jnp.float32),
                jax.ShapeDtypeStruct((1,), jnp.int32),
            ],
            compiler_params=pltpu.CompilerParams(vmem_limit_bytes=20 << 20),
            cost_estimate=pl.CostEstimate(flops=sets << 32, bytes_accessed=sets << 23, transcendentals=0),
        )(*data, *tables_of(start, stop))

    far = [shard]
    for away in range(2, blocks, 2):
        far.append(exchange(tie(shard, far[-1]), "ublk", away))
    sets = len(far)
    states = []
    for at, part in enumerate(far):
        if at > 0:
            part = tie(part, beside, above)
        beside = exchange(part, "ublk", 1)
        above = exchange(part, "salt", 2)
        if at >= LAG:
            states.append(early(at - LAG, at - LAG + 1))
            states.append(early(1, 2))
            beside = tie(beside, states[0][4], states[1][4])
            above = tie(above, states[0][4], states[1][4])
        over = exchange(beside[:half], "salt", 2)
        under = exchange(above[half:], "ublk", 1)
        if at < sets - 1:
            mine = jnp.concatenate([part, beside, above, over, under])
            own.append(mine.reshape(salts, tile, rank))
            near.append(exchange(mine, "salt", 1).reshape(salts, tile, rank))
        else:
            most = jnp.concatenate([part, beside, above])
            rest = jnp.concatenate([over, under])
            own.append(jnp.concatenate([most, rest]).reshape(salts, tile, rank))
            near.append(jnp.concatenate([exchange(most, "salt", 1), exchange(rest, "salt", 1)]).reshape(salts, tile, rank))
    for at in range(len(states), sets - 1):
        states.append(early(at, at + 1))

    capacity = blocks * slots + STEP
    out = jax.ShapeDtypeStruct((ITEM_DEV, rank), jnp.float32)
    whole = pl.BlockSpec((ITEM_DEV, rank), lambda i, p, q: (0, 0))
    before_specs = []
    for state in states:
        before_specs += [
            pl.BlockSpec(memory_space=pl.ANY),
            pl.BlockSpec(state[1].shape, lambda i, p, q: (0, 0)),
            pl.BlockSpec(state[2].shape, lambda i, p, q: (0, 0)),
            pl.BlockSpec(state[3].shape, lambda i, p, q: (0, 0)),
            pl.BlockSpec(memory_space=pltpu.SMEM),
        ]
    solution, resid = pl.pallas_call(
        functools.partial(last_kernel, 2 * (sets - 1), len(states)),
        grid_spec=pltpu.PrefetchScalarGridSpec(
            num_scalar_prefetch=2,
            grid=(2,),
            in_specs=specs(2 * (sets - 1), 1) + before_specs,
            out_specs=[whole, whole],
            scratch_shapes=[
                pltpu.VMEM((block_users, rank), jnp.float32),
                pltpu.VMEM((capacity, rank), jnp.bfloat16),
                pltpu.VMEM((capacity // LANES, LANES), jnp.int32),
                pltpu.VMEM((capacity // LANES, LANES), jnp.float32),
                pltpu.VMEM((rank, rank), jnp.float32),
                pltpu.SMEM((1,), jnp.int32),
                pltpu.SemaphoreType.DMA((8,)),
            ],
        ),
        out_shape=[out, out],
        compiler_params=pltpu.CompilerParams(vmem_limit_bytes=32 << 20),
    )(*data, *tables_of(sets - 1, sets), *[part for state in states for part in state])
    return (solution[None], resid[None])


def solution(mesh):
    def body(user_factors, *tiles):
        table_bytes = user_factors.size * mesh.size * user_factors.dtype.itemsize
        blocks = mesh.shape["ublk"]
        swaps = mesh.shape["salt"] == 4 and blocks >= 8 and blocks & (blocks - 1) == 0
        chosen = gathered_body if swaps and table_bytes <= TABLE_BYTES else reduced_body
        return chosen(user_factors, *tiles)

    return jax.shard_map(
        body,
        mesh=mesh,
        in_specs=(
            P("ublk", "salt", None),
            P("ublk", "salt", None),
            P("ublk", "salt", None),
            P("ublk", "salt", None),
            P("ublk", "salt"),
        ),
        out_specs=(P("salt", "ublk", None), P("salt", "ublk", None)),
        check_vma=False,
    )
```

```python
import functools

import jax
import jax.numpy as jnp
from jax import lax
from jax.experimental import pallas as pl
from jax.experimental.pallas import tpu as pltpu
from jax.sharding import PartitionSpec as P

ITERS = 8
ITEM_DEV = 32

REG = 1.0
EPS = 1e-06

LANES = 128
STEP = 2048
WIDE = 2
UNROLL = 128
LAG = 3
TABLE_BYTES = 1 << 25


def conjugate(rhs, image_of):
    solution = jnp.zeros_like(rhs)
    resid = rhs
    direction = rhs
    norm_now = jnp.sum(resid * resid, axis=1)
    for step in range(ITERS):
        image = image_of(direction)
        alpha = norm_now / (jnp.sum(direction * image, axis=1) + EPS)
        solution = solution + alpha[:, None] * direction
        resid = resid - alpha[:, None] * image
        norm_next = jnp.sum(resid * resid, axis=1)
        direction = resid + (norm_next / (norm_now + EPS))[:, None] * direction
        norm_now = norm_next
    return (solution, resid)


def reduced_body(user_factors, tile_users, tile_items, tile_weight, live_count):
    shard = user_factors[0]
    block = lax.all_gather(shard, "salt", axis=0, tiled=True)
    contract = (((0,), (0,)), ((), ()))
    own_gram = lax.dot_general(block, block, contract, preferred_element_type=jnp.float32)
    gram = lax.psum(own_gram, "ublk")
    users = tile_users[0, 0]
    items = tile_items[0, 0]
    raw = tile_weight[0, 0]
    live = jnp.arange(users.shape[0], dtype=jnp.int32) < live_count[0, 0]
    weight = jnp.where(live, raw, jnp.zeros_like(raw))
    confid = jnp.where(live, 1.0 + raw, jnp.zeros_like(raw))
    rows = jnp.take(block, users, axis=0).astype(jnp.float32)
    column_items = ITEM_DEV * lax.axis_size("ublk")
    rhs_terms = jax.ops.segment_sum(confid[:, None] * rows, items, num_segments=column_items)

    def local_terms(whole_dir):
        along = jnp.sum(rows * whole_dir[items], axis=1) * weight
        return jax.ops.segment_sum(along[:, None] * rows, items, num_segments=column_items)

    def finish(summed, direction):
        return summed + jnp.dot(direction, gram, precision=lax.Precision.HIGHEST) + REG * direction

    rhs = lax.psum(rhs_terms, "ublk")

    def image_every(direction):
        summed = lax.psum(local_terms(direction), "ublk")
        return finish(summed, direction)

    solution_all, resid_all = conjugate(rhs, image_every)
    start = lax.axis_index("ublk") * ITEM_DEV
    solution = lax.dynamic_slice_in_dim(solution_all, start, ITEM_DEV, 0)
    resid = lax.dynamic_slice_in_dim(resid_all, start, ITEM_DEV, 0)
    return (solution[None], resid[None])


def two_parts(value):
    high = value.astype(jnp.bfloat16)
    low = (value - high.astype(jnp.float32)).astype(jnp.bfloat16)
    return jnp.concatenate([high, low], axis=0)


def pick_rows(lo, hi, first, last, users_ref, keys_ref, weight_ref, wide, rows, item_s, weight_s, count):
    def group(j, at):
        key = keys_ref[0, pl.ds(j, 1), :]
        mine = (key >= lo) & (key < hi)
        item_s[pl.ds(at, 1), :] = jnp.where(mine, key & (ITEM_DEV - 1), -1)
        weight_s[pl.ds(at, 1), :] = jnp.where(mine, weight_ref[0, pl.ds(j, 1), :], 0.0)

        def some(i, carry):
            base = pl.multiple_of(i * UNROLL, UNROLL)
            taken = [wide[pl.ds(users_ref[0, 0, j * LANES + base + k], 1), :] for k in range(UNROLL)]
            to = pl.ds(pl.multiple_of(at * LANES + base, UNROLL), UNROLL)
            rows[to, :] = jnp.concatenate(taken, axis=0).astype(rows.dtype)
            return carry

        lax.fori_loop(0, LANES // UNROLL, some, 0)
        return at + 1

    stop = jnp.where(last > first, (last + LANES - 1) // LANES, first // LANES)
    count[0] = lax.fori_loop(first // LANES, stop, group, count[0])


def absorb(base, place_ref, bounds_ref, users_ref, keys_ref, weight_ref, pieces, wide, rows, item_s, weight_s, gram, count):
    tile = pieces[0].shape[0]
    users = tile * len(pieces)
    added = None
    for away, piece in enumerate(pieces):
        here = piece[...]
        start = pl.multiple_of((place_ref[1] ^ away) * tile, tile)
        wide[pl.ds(start, tile), :] = here.astype(jnp.float32)
        term = lax.dot_general(here, here, (((0,), (0,)), ((), ())), preferred_element_type=jnp.float32)
        added = term if added is None else added + term
    gram[...] += added
    lo = place_ref[0] * (users * ITEM_DEV)
    hi = lo + users * ITEM_DEV
    pick_rows(
        lo, hi, bounds_ref[2 * base], bounds_ref[2 * base + 1], users_ref, keys_ref, weight_ref, wide, rows, item_s, weight_s, count
    )


def pieces_of(refs):
    own_near, own_far, next_near, next_far = refs
    return [own_near.at[0], next_near.at[0], own_far.at[0], next_far.at[0]]


def early_kernel(base, sets, place_ref, bounds_ref, users_ref, keys_ref, weight_ref, *refs):
    tables, (rows_out, item_s, weight_s, gram, count), (wide, rows, sems) = refs[: 4 * sets], refs[4 * sets : -3], refs[-3:]
    step = pl.program_id(0)

    @pl.when(step == 0)
    def _():
        count[0] = 0
        gram[...] = jnp.zeros_like(gram)

    for at in range(sets):

        @pl.when(step // 2 == at)
        def _(at=at):
            absorb(
                base + step, place_ref, bounds_ref, users_ref, keys_ref, weight_ref,
                pieces_of(tables[4 * at : 4 * at + 4]), wide, rows, item_s, weight_s, gram, count,
            )

    @pl.when(step == pl.num_programs(0) - 1)
    def _():
        move_groups(rows, rows_out, 0, count[0], sems)


def move_groups(source, target, to, number, sems):
    depth = sems.shape[0]

    def copy(i):
        return pltpu.make_async_copy(
            source.at[pl.ds(pl.multiple_of(i * LANES, LANES), LANES), :],
            target.at[pl.ds(pl.multiple_of((to + i) * LANES, LANES), LANES), :],
            sems.at[i % depth],
        )

    def start(i, carry):
        @pl.when(i >= depth)
        def _():
            copy(i - depth).wait()

        copy(i).start()
        return carry

    def finish(i, carry):
        copy(i).wait()
        return carry

    lax.fori_loop(0, number, start, 0)
    lax.fori_loop(jnp.maximum(number - depth, 0), number, finish, 0)


def last_kernel(base, earlier, place_ref, bounds_ref, users_ref, keys_ref, weight_ref, *refs):
    tables, before, (solution_ref, resid_ref) = refs[:4], refs[4 : 4 + 5 * earlier], refs[4 + 5 * earlier : 6 + 5 * earlier]
    wide, rows, item_s, weight_s, gram, count, sems = refs[6 + 5 * earlier :]
    step = pl.program_id(0)

    @pl.when(step == 0)
    def _():
        gram[...] = jnp.zeros_like(gram)
        total = 0
        for at in range(earlier):
            rows_ref, item_ref, weight_in, gram_ref, count_ref = before[5 * at : 5 * at + 5]
            number = count_ref[0]
            move_groups(rows_ref, rows, total, number, sems)

            def line(i, carry, item_ref=item_ref, weight_in=weight_in, total=total):
                item_s[pl.ds(total + i, 1), :] = item_ref[pl.ds(i, 1), :]
                weight_s[pl.ds(total + i, 1), :] = weight_in[pl.ds(i, 1), :]
                return carry

            lax.fori_loop(0, number, line, 0)
            gram[...] += gram_ref[...]
            total = total + number
        count[0] = total

    absorb(
        base + step, place_ref, bounds_ref, users_ref, keys_ref, weight_ref,
        pieces_of(tables), wide, rows, item_s, weight_s, gram, count,
    )

    @pl.when(step == pl.num_programs(0) - 1)
    def _():
        solve_items(rows, item_s, weight_s, count, gram, solution_ref, resid_ref)


def solve_items(rows, item_s, weight_s, count, gram, solution_ref, resid_ref):
    groups = STEP // LANES
    filled = count[0]
    steps = (filled + groups - 1) // groups

    def clear(at, carry):
        rows[pl.ds(pl.multiple_of(at * LANES, LANES), LANES), :] = jnp.zeros((LANES, rows.shape[1]), rows.dtype)
        item_s[pl.ds(at, 1), :] = jnp.full((1, LANES), -1, jnp.int32)
        weight_s[pl.ds(at, 1), :] = jnp.zeros((1, LANES), jnp.float32)
        return carry

    lax.fori_loop(filled, steps * groups, clear, 0)
    own = lax.broadcasted_iota(jnp.int32, (ITEM_DEV, STEP), 0)

    def along(ref, step):
        return jnp.concatenate([ref[pl.ds(step * groups + g, 1), :] for g in range(groups)], axis=1)

    def held(step):
        return rows[pl.ds(pl.multiple_of(step * STEP, STEP), STEP), :]

    def halves(pair):
        return pair[:ITEM_DEV] + pair[ITEM_DEV:]

    def summed(term):
        acc = jnp.zeros((2 * ITEM_DEV, rows.shape[1]), jnp.float32)

        done = 0
        for wide in (4, 2, 1):

            def many(i, acc, wide=wide, done=done):
                for k in range(wide):
                    acc = acc + term(done + i * wide + k)
                return acc

            turns = (steps - done) // wide
            acc = lax.fori_loop(0, turns, many, acc)
            done = done + turns * wide
        return halves(acc)

    def rhs_term(step):
        scaled = jnp.where(along(item_s, step) == own, 1.0 + along(weight_s, step), 0.0)
        return jnp.dot(two_parts(scaled), held(step), preferred_element_type=jnp.float32)

    rhs = summed(rhs_term)

    def image_of(direction):
        parts = two_parts(direction)

        def term(step):
            here = held(step)
            dots = lax.dot_general(parts, here, (((1,), (1,)), ((), ())), preferred_element_type=jnp.float32)
            scaled = jnp.where(along(item_s, step) == own, halves(dots) * along(weight_s, step), 0.0)
            return jnp.dot(two_parts(scaled), here, preferred_element_type=jnp.float32)

        return summed(term) + jnp.dot(direction, gram[...], precision=lax.Precision.HIGHEST) + REG * direction

    def iterate(_, state):
        solution, resid, direction, norm_now = state
        image = image_of(direction)
        alpha = norm_now / (jnp.sum(direction * image, axis=1, keepdims=True) + EPS)
        solution = solution + alpha * direction
        resid = resid - alpha * image
        norm_next = jnp.sum(resid * resid, axis=1, keepdims=True)
        direction = resid + (norm_next / (norm_now + EPS)) * direction
        return (solution, resid, direction, norm_next)

    state = (jnp.zeros_like(rhs), rhs, rhs, jnp.sum(rhs * rhs, axis=1, keepdims=True))
    solution, resid, _, _ = lax.fori_loop(0, ITERS, iterate, state)
    solution_ref[...] = solution
    resid_ref[...] = resid


def exchange(value, axis, away):
    return lax.ppermute(value, axis, [(i, i ^ away) for i in range(lax.axis_size(axis))])


def tie(value, *others):
    return lax.optimization_barrier((value, *others))[0]


def gathered_body(user_factors, tile_users, tile_items, tile_weight, live_count):
    shard = user_factors[0]
    blocks = lax.axis_size("ublk")
    salts = lax.axis_size("salt")
    tile, rank = shard.shape
    block_users = tile * salts
    slots = tile_users.shape[2]
    lines = slots // LANES
    live = jnp.arange(slots, dtype=jnp.int32) < live_count[0, 0]
    items = tile_items[0, 0]
    key = ((items // ITEM_DEV) * block_users + tile_users[0, 0]) * ITEM_DEV + items % ITEM_DEV
    key = jnp.where(live, key, blocks * block_users * ITEM_DEV)
    key, weight = lax.sort((key, tile_weight[0, 0]), num_keys=1, is_stable=False)
    meta = jnp.stack([key.astype(jnp.float32), weight])[None]
    meta = jnp.concatenate([meta, exchange(meta, "ublk", 1)])
    meta = jnp.concatenate([meta] + [exchange(meta, "ublk", away) for away in range(2, blocks, 2)])
    keys = meta[:, 0].astype(jnp.int32)
    weights = meta[:, 1].reshape(blocks, lines, LANES)
    me = lax.axis_index("ublk").astype(jnp.int32)
    lo = me * (block_users * ITEM_DEV)
    hi = lo + block_users * ITEM_DEV
    bounds = jnp.stack([jnp.sum((keys < lo).astype(jnp.int32), axis=1), jnp.sum((keys < hi).astype(jnp.int32), axis=1)], axis=1)
    users = jnp.clip((keys - lo) // ITEM_DEV, 0, block_users - 1).reshape(blocks, 1, slots)
    place = jnp.stack([me, lax.axis_index("salt").astype(jnp.int32)])
    data = (place, bounds.reshape(-1), users, keys.reshape(blocks, lines, LANES), weights)

    half = tile // 2
    near = []
    own = []

    def specs(base, sets):
        def block_at(i, place_ref, _):
            return (base + i, 0, 0)

        tables = []
        for at in range(sets):
            for _ in range(2):
                for row in range(2):
                    tables.append(
                        pl.BlockSpec((1, tile, rank), lambda i, p, q, at=at, row=row: (2 * row + jnp.clip(i - 2 * at, 0, 1), 0, 0))
                    )
        return [
            pl.BlockSpec((1, 1, slots), block_at, memory_space=pltpu.SMEM),
            pl.BlockSpec((1, lines, LANES), block_at),
            pl.BlockSpec((1, lines, LANES), block_at),
            *tables,
        ]

    def tables_of(start, stop):
        return [part for at in range(start, stop) for part in (own[at], own[at], near[at], near[at])]

    def early(start, stop):
        sets = stop - start
        capacity = 2 * sets * slots
        fixed = lambda i, p, q: (0, 0)
        return pl.pallas_call(
            functools.partial(early_kernel, 2 * start, sets),
            grid_spec=pltpu.PrefetchScalarGridSpec(
                num_scalar_prefetch=2,
                grid=(2 * sets,),
                in_specs=specs(2 * start, sets),
                out_specs=[
                    pl.BlockSpec(memory_space=pl.ANY),
                    pl.BlockSpec((capacity // LANES, LANES), fixed),
                    pl.BlockSpec((capacity // LANES, LANES), fixed),
                    pl.BlockSpec((rank, rank), fixed),
                    pl.BlockSpec(memory_space=pltpu.SMEM),
                ],
                scratch_shapes=[
                    pltpu.VMEM((block_users, rank), jnp.float32),
                    pltpu.VMEM((capacity, rank), jnp.bfloat16),
                    pltpu.SemaphoreType.DMA((8,)),
                ],
            ),
            out_shape=[
                jax.ShapeDtypeStruct((capacity, rank), jnp.bfloat16),
                jax.ShapeDtypeStruct((capacity // LANES, LANES), jnp.int32),
                jax.ShapeDtypeStruct((capacity // LANES, LANES), jnp.float32),
                jax.ShapeDtypeStruct((rank, rank), jnp.float32),
                jax.ShapeDtypeStruct((1,), jnp.int32),
            ],
            compiler_params=pltpu.CompilerParams(vmem_limit_bytes=20 << 20),
            cost_estimate=pl.CostEstimate(flops=sets << 32, bytes_accessed=sets << 23, transcendentals=0),
        )(*data, *tables_of(start, stop))

    far = [shard]
    for away in range(2, blocks, 2):
        far.append(exchange(tie(shard, far[-1]), "ublk", away))
    sets = len(far)
    states = []
    for at, part in enumerate(far):
        if at > 0:
            part = tie(part, beside, above)
        beside = exchange(part, "ublk", 1)
        above = exchange(part, "salt", 2)
        if at >= LAG:
            states.append(early(at - LAG, at - LAG + 1))
            states.append(early(1, 2))
            beside = tie(beside, states[0][4], states[1][4])
            above = tie(above, states[0][4], states[1][4])
        over = exchange(beside[:half], "salt", 2)
        under = exchange(above[half:], "ublk", 1)
        if at < sets - 1:
            mine = jnp.concatenate([part, beside, above, over, under])
            own.append(mine.reshape(salts, tile, rank))
            near.append(exchange(mine, "salt", 1).reshape(salts, tile, rank))
        else:
            most = jnp.concatenate([part, beside, above])
            rest = jnp.concatenate([over, under])
            own.append(jnp.concatenate([most, rest]).reshape(salts, tile, rank))
            near.append(jnp.concatenate([exchange(most, "salt", 1), exchange(rest, "salt", 1)]).reshape(salts, tile, rank))
    for at in range(len(states), sets - 1):
        states.append(early(at, at + 1))

    capacity = blocks * slots + STEP
    out = jax.ShapeDtypeStruct((ITEM_DEV, rank), jnp.float32)
    whole = pl.BlockSpec((ITEM_DEV, rank), lambda i, p, q: (0, 0))
    before_specs = []
    for state in states:
        before_specs += [
            pl.BlockSpec(memory_space=pl.ANY),
            pl.BlockSpec(state[1].shape, lambda i, p, q: (0, 0)),
            pl.BlockSpec(state[2].shape, lambda i, p, q: (0, 0)),
            pl.BlockSpec(state[3].shape, lambda i, p, q: (0, 0)),
            pl.BlockSpec(memory_space=pltpu.SMEM),
        ]
    solution, resid = pl.pallas_call(
        functools.partial(last_kernel, 2 * (sets - 1), len(states)),
        grid_spec=pltpu.PrefetchScalarGridSpec(
            num_scalar_prefetch=2,
            grid=(2,),
            in_specs=specs(2 * (sets - 1), 1) + before_specs,
            out_specs=[whole, whole],
            scratch_shapes=[
                pltpu.VMEM((block_users, rank), jnp.float32),
                pltpu.VMEM((capacity, rank), jnp.bfloat16),
                pltpu.VMEM((capacity // LANES, LANES), jnp.int32),
                pltpu.VMEM((capacity // LANES, LANES), jnp.float32),
                pltpu.VMEM((rank, rank), jnp.float32),
                pltpu.SMEM((1,), jnp.int32),
                pltpu.SemaphoreType.DMA((8,)),
            ],
        ),
        out_shape=[out, out],
        compiler_params=pltpu.CompilerParams(vmem_limit_bytes=32 << 20),
    )(*data, *tables_of(sets - 1, sets), *[part for state in states for part in state])
    return (solution[None], resid[None])


def solution(mesh):
    def body(user_factors, *tiles):
        table_bytes = user_factors.size * mesh.size * user_factors.dtype.itemsize
        blocks = mesh.shape["ublk"]
        swaps = mesh.shape["salt"] == 4 and blocks >= 8 and blocks & (blocks - 1) == 0
        chosen = gathered_body if swaps and table_bytes <= TABLE_BYTES else reduced_body
        return chosen(user_factors, *tiles)

    return jax.shard_map(
        body,
        mesh=mesh,
        in_specs=(
            P("ublk", "salt", None),
            P("ublk", "salt", None),
            P("ublk", "salt", None),
            P("ublk", "salt", None),
            P("ublk", "salt"),
        ),
        out_specs=(P("salt", "ublk", None), P("salt", "ublk", None)),
        check_vma=False,
    )
```

```python
import functools

import jax
import jax.numpy as jnp
from jax import lax
from jax.experimental import pallas as pl
from jax.experimental.pallas import tpu as pltpu
from jax.sharding import PartitionSpec as P

ITERS = 8
ITEM_DEV = 32

REG = 1.0
EPS = 1e-06

LANES = 128
STEP = 2048
WIDE = 2
UNROLL = 128
LAG = 3
TABLE_BYTES = 1 << 25


def conjugate(rhs, image_of):
    solution = jnp.zeros_like(rhs)
    resid = rhs
    direction = rhs
    norm_now = jnp.sum(resid * resid, axis=1)
    for step in range(ITERS):
        image = image_of(direction)
        alpha = norm_now / (jnp.sum(direction * image, axis=1) + EPS)
        solution = solution + alpha[:, None] * direction
        resid = resid - alpha[:, None] * image
        norm_next = jnp.sum(resid * resid, axis=1)
        direction = resid + (norm_next / (norm_now + EPS))[:, None] * direction
        norm_now = norm_next
    return (solution, resid)


def reduced_body(user_factors, tile_users, tile_items, tile_weight, live_count):
    shard = user_factors[0]
    block = lax.all_gather(shard, "salt", axis=0, tiled=True)
    contract = (((0,), (0,)), ((), ()))
    own_gram = lax.dot_general(block, block, contract, preferred_element_type=jnp.float32)
    gram = lax.psum(own_gram, "ublk")
    users = tile_users[0, 0]
    items = tile_items[0, 0]
    raw = tile_weight[0, 0]
    live = jnp.arange(users.shape[0], dtype=jnp.int32) < live_count[0, 0]
    weight = jnp.where(live, raw, jnp.zeros_like(raw))
    confid = jnp.where(live, 1.0 + raw, jnp.zeros_like(raw))
    rows = jnp.take(block, users, axis=0).astype(jnp.float32)
    column_items = ITEM_DEV * lax.axis_size("ublk")
    rhs_terms = jax.ops.segment_sum(confid[:, None] * rows, items, num_segments=column_items)

    def local_terms(whole_dir):
        along = jnp.sum(rows * whole_dir[items], axis=1) * weight
        return jax.ops.segment_sum(along[:, None] * rows, items, num_segments=column_items)

    def finish(summed, direction):
        return summed + jnp.dot(direction, gram, precision=lax.Precision.HIGHEST) + REG * direction

    rhs = lax.psum(rhs_terms, "ublk")

    def image_every(direction):
        summed = lax.psum(local_terms(direction), "ublk")
        return finish(summed, direction)

    solution_all, resid_all = conjugate(rhs, image_every)
    start = lax.axis_index("ublk") * ITEM_DEV
    solution = lax.dynamic_slice_in_dim(solution_all, start, ITEM_DEV, 0)
    resid = lax.dynamic_slice_in_dim(resid_all, start, ITEM_DEV, 0)
    return (solution[None], resid[None])


def two_parts(value):
    high = value.astype(jnp.bfloat16)
    low = (value - high.astype(jnp.float32)).astype(jnp.bfloat16)
    return jnp.concatenate([high, low], axis=0)


def three_parts(value):
    high = value.astype(jnp.bfloat16)
    rest = value - high.astype(jnp.float32)
    middle = rest.astype(jnp.bfloat16)
    return [high, middle, (rest - middle.astype(jnp.float32)).astype(jnp.bfloat16)]


def pick_rows(lo, hi, first, last, users_ref, keys_ref, weight_ref, wide, rows, item_s, weight_s, count):
    def group(j, at):
        key = keys_ref[0, pl.ds(j, 1), :]
        mine = (key >= lo) & (key < hi)
        item_s[pl.ds(at, 1), :] = jnp.where(mine, key & (ITEM_DEV - 1), -1)
        weight_s[pl.ds(at, 1), :] = jnp.where(mine, weight_ref[0, pl.ds(j, 1), :], 0.0)

        def some(i, carry):
            base = pl.multiple_of(i * UNROLL, UNROLL)
            taken = [wide[pl.ds(users_ref[0, 0, j * LANES + base + k], 1), :] for k in range(UNROLL)]
            to = pl.ds(pl.multiple_of(at * LANES + base, UNROLL), UNROLL)
            rows[to, :] = jnp.concatenate(taken, axis=0).astype(rows.dtype)
            return carry

        lax.fori_loop(0, LANES // UNROLL, some, 0)
        return at + 1

    stop = jnp.where(last > first, (last + LANES - 1) // LANES, first // LANES)
    count[0] = lax.fori_loop(first // LANES, stop, group, count[0])


def absorb(base, place_ref, bounds_ref, users_ref, keys_ref, weight_ref, pieces, wide, rows, item_s, weight_s, gram, count):
    tile = pieces[0].shape[0]
    users = tile * len(pieces)
    added = None
    for away, piece in enumerate(pieces):
        here = piece[...]
        start = pl.multiple_of((place_ref[1] ^ away) * tile, tile)
        wide[pl.ds(start, tile), :] = here.astype(jnp.float32)
        term = lax.dot_general(here, here, (((0,), (0,)), ((), ())), preferred_element_type=jnp.float32)
        added = term if added is None else added + term
    gram[...] += added
    lo = place_ref[0] * (users * ITEM_DEV)
    hi = lo + users * ITEM_DEV
    pick_rows(
        lo, hi, bounds_ref[2 * base], bounds_ref[2 * base + 1], users_ref, keys_ref, weight_ref, wide, rows, item_s, weight_s, count
    )


def pieces_of(refs):
    own_near, own_far, next_near, next_far = refs
    return [own_near.at[0], next_near.at[0], own_far.at[0], next_far.at[0]]


def early_kernel(base, sets, place_ref, bounds_ref, users_ref, keys_ref, weight_ref, *refs):
    tables, (rows_out, item_s, weight_s, gram, count), (wide, rows, sems) = refs[: 4 * sets], refs[4 * sets : -3], refs[-3:]
    step = pl.program_id(0)

    @pl.when(step == 0)
    def _():
        count[0] = 0
        gram[...] = jnp.zeros_like(gram)

    for at in range(sets):

        @pl.when(step // 2 == at)
        def _(at=at):
            absorb(
                base + step, place_ref, bounds_ref, users_ref, keys_ref, weight_ref,
                pieces_of(tables[4 * at : 4 * at + 4]), wide, rows, item_s, weight_s, gram, count,
            )

    @pl.when(step == pl.num_programs(0) - 1)
    def _():
        move_groups(rows, rows_out, 0, count[0], sems)


def move_groups(source, target, to, number, sems):
    depth = sems.shape[0]

    def copy(i):
        return pltpu.make_async_copy(
            source.at[pl.ds(pl.multiple_of(i * LANES, LANES), LANES), :],
            target.at[pl.ds(pl.multiple_of((to + i) * LANES, LANES), LANES), :],
            sems.at[i % depth],
        )

    def start(i, carry):
        @pl.when(i >= depth)
        def _():
            copy(i - depth).wait()

        copy(i).start()
        return carry

    def finish(i, carry):
        copy(i).wait()
        return carry

    lax.fori_loop(0, number, start, 0)
    lax.fori_loop(jnp.maximum(number - depth, 0), number, finish, 0)


def last_kernel(base, earlier, place_ref, bounds_ref, users_ref, keys_ref, weight_ref, *refs):
    tables, before, (solution_ref, resid_ref) = refs[:4], refs[4 : 4 + 5 * earlier], refs[4 + 5 * earlier : 6 + 5 * earlier]
    wide, rows, item_s, weight_s, gram, count, sems = refs[6 + 5 * earlier :]
    step = pl.program_id(0)

    @pl.when(step == 0)
    def _():
        gram[...] = jnp.zeros_like(gram)
        total = 0
        for at in range(earlier):
            rows_ref, item_ref, weight_in, gram_ref, count_ref = before[5 * at : 5 * at + 5]
            number = count_ref[0]
            move_groups(rows_ref, rows, total, number, sems)

            def line(i, carry, item_ref=item_ref, weight_in=weight_in, total=total):
                item_s[pl.ds(total + i, 1), :] = item_ref[pl.ds(i, 1), :]
                weight_s[pl.ds(total + i, 1), :] = weight_in[pl.ds(i, 1), :]
                return carry

            lax.fori_loop(0, number, line, 0)
            gram[...] += gram_ref[...]
            total = total + number
        count[0] = total

    absorb(
        base + step, place_ref, bounds_ref, users_ref, keys_ref, weight_ref,
        pieces_of(tables), wide, rows, item_s, weight_s, gram, count,
    )

    @pl.when(step == pl.num_programs(0) - 1)
    def _():
        solve_items(rows, item_s, weight_s, count, gram, solution_ref, resid_ref)


def solve_items(rows, item_s, weight_s, count, gram, solution_ref, resid_ref):
    groups = STEP // LANES
    filled = count[0]
    steps = (filled + groups - 1) // groups

    def clear(at, carry):
        rows[pl.ds(pl.multiple_of(at * LANES, LANES), LANES), :] = jnp.zeros((LANES, rows.shape[1]), rows.dtype)
        item_s[pl.ds(at, 1), :] = jnp.full((1, LANES), -1, jnp.int32)
        weight_s[pl.ds(at, 1), :] = jnp.zeros((1, LANES), jnp.float32)
        return carry

    lax.fori_loop(filled, steps * groups, clear, 0)
    own = lax.broadcasted_iota(jnp.int32, (ITEM_DEV, STEP), 0)

    def along(ref, step):
        return jnp.concatenate([ref[pl.ds(step * groups + g, 1), :] for g in range(groups)], axis=1)

    def held(step):
        return rows[pl.ds(pl.multiple_of(step * STEP, STEP), STEP), :]

    def halves(pair):
        return pair[:ITEM_DEV] + pair[ITEM_DEV:]

    def summed(term):
        acc = jnp.zeros((2 * ITEM_DEV, rows.shape[1]), jnp.float32)

        done = 0
        for wide in (4, 2, 1):

            def many(i, acc, wide=wide, done=done):
                for k in range(wide):
                    acc = acc + term(done + i * wide + k)
                return acc

            turns = (steps - done) // wide
            acc = lax.fori_loop(0, turns, many, acc)
            done = done + turns * wide
        return halves(acc)

    def rhs_term(step):
        scaled = jnp.where(along(item_s, step) == own, 1.0 + along(weight_s, step), 0.0)
        return jnp.dot(two_parts(scaled), held(step), preferred_element_type=jnp.float32)

    rhs = summed(rhs_term)

    squares = three_parts(gram[...])

    def by_gram(split):
        added = None
        for k, square in enumerate(squares):
            many = jnp.dot(jnp.concatenate(split[: 3 - k], axis=0), square, preferred_element_type=jnp.float32)
            for start in range(0, many.shape[0], ITEM_DEV):
                piece = many[start : start + ITEM_DEV]
                added = piece if added is None else added + piece
        return added

    def image_of(direction):
        split = three_parts(direction)
        parts = jnp.concatenate(split[:2], axis=0)

        def term(step):
            here = held(step)
            dots = lax.dot_general(parts, here, (((1,), (1,)), ((), ())), preferred_element_type=jnp.float32)
            scaled = jnp.where(along(item_s, step) == own, halves(dots) * along(weight_s, step), 0.0)
            return jnp.dot(two_parts(scaled), here, preferred_element_type=jnp.float32)

        return summed(term) + by_gram(split) + REG * direction

    def iterate(_, state):
        solution, resid, direction, norm_now = state
        image = image_of(direction)
        alpha = norm_now / (jnp.sum(direction * image, axis=1, keepdims=True) + EPS)
        solution = solution + alpha * direction
        resid = resid - alpha * image
        norm_next = jnp.sum(resid * resid, axis=1, keepdims=True)
        direction = resid + (norm_next / (norm_now + EPS)) * direction
        return (solution, resid, direction, norm_next)

    state = (jnp.zeros_like(rhs), rhs, rhs, jnp.sum(rhs * rhs, axis=1, keepdims=True))
    solution, resid, _, _ = lax.fori_loop(0, ITERS, iterate, state)
    solution_ref[...] = solution
    resid_ref[...] = resid


def exchange(value, axis, away):
    return lax.ppermute(value, axis, [(i, i ^ away) for i in range(lax.axis_size(axis))])


def tie(value, *others):
    return lax.optimization_barrier((value, *others))[0]


def gathered_body(user_factors, tile_users, tile_items, tile_weight, live_count):
    shard = user_factors[0]
    blocks = lax.axis_size("ublk")
    salts = lax.axis_size("salt")
    tile, rank = shard.shape
    block_users = tile * salts
    slots = tile_users.shape[2]
    lines = slots // LANES
    live = jnp.arange(slots, dtype=jnp.int32) < live_count[0, 0]
    items = tile_items[0, 0]
    key = ((items // ITEM_DEV) * block_users + tile_users[0, 0]) * ITEM_DEV + items % ITEM_DEV
    key = jnp.where(live, key, blocks * block_users * ITEM_DEV)
    key, weight = lax.sort((key, tile_weight[0, 0]), num_keys=1, is_stable=False)
    meta = jnp.stack([key.astype(jnp.float32), weight])[None]
    meta = jnp.concatenate([meta, exchange(meta, "ublk", 1)])
    meta = jnp.concatenate([meta] + [exchange(meta, "ublk", away) for away in range(2, blocks, 2)])
    keys = meta[:, 0].astype(jnp.int32)
    weights = meta[:, 1].reshape(blocks, lines, LANES)
    me = lax.axis_index("ublk").astype(jnp.int32)
    lo = me * (block_users * ITEM_DEV)
    hi = lo + block_users * ITEM_DEV
    bounds = jnp.stack([jnp.sum((keys < lo).astype(jnp.int32), axis=1), jnp.sum((keys < hi).astype(jnp.int32), axis=1)], axis=1)
    users = jnp.clip((keys - lo) // ITEM_DEV, 0, block_users - 1).reshape(blocks, 1, slots)
    place = jnp.stack([me, lax.axis_index("salt").astype(jnp.int32)])
    data = (place, bounds.reshape(-1), users, keys.reshape(blocks, lines, LANES), weights)

    half = tile // 2
    near = []
    own = []

    def specs(base, sets):
        def block_at(i, place_ref, _):
            return (base + i, 0, 0)

        tables = []
        for at in range(sets):
            for _ in range(2):
                for row in range(2):
                    tables.append(
                        pl.BlockSpec((1, tile, rank), lambda i, p, q, at=at, row=row: (2 * row + jnp.clip(i - 2 * at, 0, 1), 0, 0))
                    )
        return [
            pl.BlockSpec((1, 1, slots), block_at, memory_space=pltpu.SMEM),
            pl.BlockSpec((1, lines, LANES), block_at),
            pl.BlockSpec((1, lines, LANES), block_at),
            *tables,
        ]

    def tables_of(start, stop):
        return [part for at in range(start, stop) for part in (own[at], own[at], near[at], near[at])]

    def early(start, stop):
        sets = stop - start
        capacity = 2 * sets * slots
        fixed = lambda i, p, q: (0, 0)
        return pl.pallas_call(
            functools.partial(early_kernel, 2 * start, sets),
            grid_spec=pltpu.PrefetchScalarGridSpec(
                num_scalar_prefetch=2,
                grid=(2 * sets,),
                in_specs=specs(2 * start, sets),
                out_specs=[
                    pl.BlockSpec(memory_space=pl.ANY),
                    pl.BlockSpec((capacity // LANES, LANES), fixed),
                    pl.BlockSpec((capacity // LANES, LANES), fixed),
                    pl.BlockSpec((rank, rank), fixed),
                    pl.BlockSpec(memory_space=pltpu.SMEM),
                ],
                scratch_shapes=[
                    pltpu.VMEM((block_users, rank), jnp.float32),
                    pltpu.VMEM((capacity, rank), jnp.bfloat16),
                    pltpu.SemaphoreType.DMA((8,)),
                ],
            ),
            out_shape=[
                jax.ShapeDtypeStruct((capacity, rank), jnp.bfloat16),
                jax.ShapeDtypeStruct((capacity // LANES, LANES), jnp.int32),
                jax.ShapeDtypeStruct((capacity // LANES, LANES), jnp.float32),
                jax.ShapeDtypeStruct((rank, rank), jnp.float32),
                jax.ShapeDtypeStruct((1,), jnp.int32),
            ],
            compiler_params=pltpu.CompilerParams(vmem_limit_bytes=20 << 20),
            cost_estimate=pl.CostEstimate(flops=sets << 32, bytes_accessed=sets << 23, transcendentals=0),
        )(*data, *tables_of(start, stop))

    far = [shard]
    for away in range(2, blocks, 2):
        far.append(exchange(tie(shard, far[-1]), "ublk", away))
    sets = len(far)
    states = []
    for at, part in enumerate(far):
        if at > 0:
            part = tie(part, beside, above)
        beside = exchange(part, "ublk", 1)
        above = exchange(part, "salt", 2)
        if at >= LAG:
            states.append(early(at - LAG, at - LAG + 1))
            states.append(early(1, 2))
            beside = tie(beside, states[0][4], states[1][4])
            above = tie(above, states[0][4], states[1][4])
        over = exchange(beside[:half], "salt", 2)
        under = exchange(above[half:], "ublk", 1)
        if at < sets - 1:
            mine = jnp.concatenate([part, beside, above, over, under])
            own.append(mine.reshape(salts, tile, rank))
            near.append(exchange(mine, "salt", 1).reshape(salts, tile, rank))
        else:
            most = jnp.concatenate([part, beside, above])
            rest = jnp.concatenate([over, under])
            own.append(jnp.concatenate([most, rest]).reshape(salts, tile, rank))
            near.append(jnp.concatenate([exchange(most, "salt", 1), exchange(rest, "salt", 1)]).reshape(salts, tile, rank))
    for at in range(len(states), sets - 1):
        states.append(early(at, at + 1))

    capacity = blocks * slots + STEP
    out = jax.ShapeDtypeStruct((ITEM_DEV, rank), jnp.float32)
    whole = pl.BlockSpec((ITEM_DEV, rank), lambda i, p, q: (0, 0))
    before_specs = []
    for state in states:
        before_specs += [
            pl.BlockSpec(memory_space=pl.ANY),
            pl.BlockSpec(state[1].shape, lambda i, p, q: (0, 0)),
            pl.BlockSpec(state[2].shape, lambda i, p, q: (0, 0)),
            pl.BlockSpec(state[3].shape, lambda i, p, q: (0, 0)),
            pl.BlockSpec(memory_space=pltpu.SMEM),
        ]
    solution, resid = pl.pallas_call(
        functools.partial(last_kernel, 2 * (sets - 1), len(states)),
        grid_spec=pltpu.PrefetchScalarGridSpec(
            num_scalar_prefetch=2,
            grid=(2,),
            in_specs=specs(2 * (sets - 1), 1) + before_specs,
            out_specs=[whole, whole],
            scratch_shapes=[
                pltpu.VMEM((block_users, rank), jnp.float32),
                pltpu.VMEM((capacity, rank), jnp.bfloat16),
                pltpu.VMEM((capacity // LANES, LANES), jnp.int32),
                pltpu.VMEM((capacity // LANES, LANES), jnp.float32),
                pltpu.VMEM((rank, rank), jnp.float32),
                pltpu.SMEM((1,), jnp.int32),
                pltpu.SemaphoreType.DMA((8,)),
            ],
        ),
        out_shape=[out, out],
        compiler_params=pltpu.CompilerParams(vmem_limit_bytes=32 << 20),
    )(*data, *tables_of(sets - 1, sets), *[part for state in states for part in state])
    return (solution[None], resid[None])


def solution(mesh):
    def body(user_factors, *tiles):
        table_bytes = user_factors.size * mesh.size * user_factors.dtype.itemsize
        blocks = mesh.shape["ublk"]
        swaps = mesh.shape["salt"] == 4 and blocks >= 8 and blocks & (blocks - 1) == 0
        chosen = gathered_body if swaps and table_bytes <= TABLE_BYTES else reduced_body
        return chosen(user_factors, *tiles)

    return jax.shard_map(
        body,
        mesh=mesh,
        in_specs=(
            P("ublk", "salt", None),
            P("ublk", "salt", None),
            P("ublk", "salt", None),
            P("ublk", "salt", None),
            P("ublk", "salt"),
        ),
        out_specs=(P("salt", "ublk", None), P("salt", "ublk", None)),
        check_vma=False,
    )
```

```python
import functools

import jax
import jax.numpy as jnp
from jax import lax
from jax.experimental import pallas as pl
from jax.experimental.pallas import tpu as pltpu
from jax.sharding import PartitionSpec as P

ITERS = 8
ITEM_DEV = 32

REG = 1.0
EPS = 1e-06

LANES = 128
STEP = 2048
WIDE = 2
UNROLL = 128
LAG = 3
TABLE_BYTES = 1 << 25


def conjugate(rhs, image_of):
    solution = jnp.zeros_like(rhs)
    resid = rhs
    direction = rhs
    norm_now = jnp.sum(resid * resid, axis=1)
    for step in range(ITERS):
        image = image_of(direction)
        alpha = norm_now / (jnp.sum(direction * image, axis=1) + EPS)
        solution = solution + alpha[:, None] * direction
        resid = resid - alpha[:, None] * image
        norm_next = jnp.sum(resid * resid, axis=1)
        direction = resid + (norm_next / (norm_now + EPS))[:, None] * direction
        norm_now = norm_next
    return (solution, resid)


def reduced_body(user_factors, tile_users, tile_items, tile_weight, live_count):
    shard = user_factors[0]
    block = lax.all_gather(shard, "salt", axis=0, tiled=True)
    contract = (((0,), (0,)), ((), ()))
    own_gram = lax.dot_general(block, block, contract, preferred_element_type=jnp.float32)
    gram = lax.psum(own_gram, "ublk")
    users = tile_users[0, 0]
    items = tile_items[0, 0]
    raw = tile_weight[0, 0]
    live = jnp.arange(users.shape[0], dtype=jnp.int32) < live_count[0, 0]
    weight = jnp.where(live, raw, jnp.zeros_like(raw))
    confid = jnp.where(live, 1.0 + raw, jnp.zeros_like(raw))
    rows = jnp.take(block, users, axis=0).astype(jnp.float32)
    column_items = ITEM_DEV * lax.axis_size("ublk")
    rhs_terms = jax.ops.segment_sum(confid[:, None] * rows, items, num_segments=column_items)

    def local_terms(whole_dir):
        along = jnp.sum(rows * whole_dir[items], axis=1) * weight
        return jax.ops.segment_sum(along[:, None] * rows, items, num_segments=column_items)

    def finish(summed, direction):
        return summed + jnp.dot(direction, gram, precision=lax.Precision.HIGHEST) + REG * direction

    rhs = lax.psum(rhs_terms, "ublk")

    def image_every(direction):
        summed = lax.psum(local_terms(direction), "ublk")
        return finish(summed, direction)

    solution_all, resid_all = conjugate(rhs, image_every)
    start = lax.axis_index("ublk") * ITEM_DEV
    solution = lax.dynamic_slice_in_dim(solution_all, start, ITEM_DEV, 0)
    resid = lax.dynamic_slice_in_dim(resid_all, start, ITEM_DEV, 0)
    return (solution[None], resid[None])


def two_parts(value):
    high = value.astype(jnp.bfloat16)
    low = (value - high.astype(jnp.float32)).astype(jnp.bfloat16)
    return jnp.concatenate([high, low], axis=0)


def three_parts(value):
    high = value.astype(jnp.bfloat16)
    rest = value - high.astype(jnp.float32)
    middle = rest.astype(jnp.bfloat16)
    return [high, middle, (rest - middle.astype(jnp.float32)).astype(jnp.bfloat16)]


def pick_rows(lo, hi, first, last, users_ref, keys_ref, weight_ref, wide, rows, item_s, weight_s, count):
    def group(j, at):
        key = keys_ref[0, pl.ds(j, 1), :]
        mine = (key >= lo) & (key < hi)
        item_s[pl.ds(at, 1), :] = jnp.where(mine, key & (ITEM_DEV - 1), -1)
        weight_s[pl.ds(at, 1), :] = jnp.where(mine, weight_ref[0, pl.ds(j, 1), :], 0.0)

        def some(i, carry):
            base = pl.multiple_of(i * UNROLL, UNROLL)
            taken = [wide[pl.ds(users_ref[0, 0, j * LANES + base + k], 1), :] for k in range(UNROLL)]
            to = pl.ds(pl.multiple_of(at * LANES + base, UNROLL), UNROLL)
            rows[to, :] = jnp.concatenate(taken, axis=0).astype(rows.dtype)
            return carry

        lax.fori_loop(0, LANES // UNROLL, some, 0)
        return at + 1

    stop = jnp.where(last > first, (last + LANES - 1) // LANES, first // LANES)
    count[0] = lax.fori_loop(first // LANES, stop, group, count[0])


def absorb(base, place_ref, bounds_ref, users_ref, keys_ref, weight_ref, pieces, wide, rows, item_s, weight_s, gram, count):
    tile = pieces[0].shape[0]
    users = tile * len(pieces)
    added = None
    for away, piece in enumerate(pieces):
        here = piece[...]
        start = pl.multiple_of((place_ref[1] ^ away) * tile, tile)
        wide[pl.ds(start, tile), :] = here.astype(jnp.float32)
        term = lax.dot_general(here, here, (((0,), (0,)), ((), ())), preferred_element_type=jnp.float32)
        added = term if added is None else added + term
    gram[...] += added
    lo = place_ref[0] * (users * ITEM_DEV)
    hi = lo + users * ITEM_DEV
    pick_rows(
        lo, hi, bounds_ref[2 * base], bounds_ref[2 * base + 1], users_ref, keys_ref, weight_ref, wide, rows, item_s, weight_s, count
    )


def pieces_of(refs):
    own_near, own_far, next_near, next_far = refs
    return [own_near.at[0], next_near.at[0], own_far.at[0], next_far.at[0]]


def early_kernel(base, sets, place_ref, bounds_ref, users_ref, keys_ref, weight_ref, *refs):
    tables, (rows_out, item_s, weight_s, gram, count), (wide, rows, sems) = refs[: 4 * sets], refs[4 * sets : -3], refs[-3:]
    step = pl.program_id(0)

    @pl.when(step == 0)
    def _():
        count[0] = 0
        gram[...] = jnp.zeros_like(gram)

    for at in range(sets):

        @pl.when(step // 2 == at)
        def _(at=at):
            absorb(
                base + step, place_ref, bounds_ref, users_ref, keys_ref, weight_ref,
                pieces_of(tables[4 * at : 4 * at + 4]), wide, rows, item_s, weight_s, gram, count,
            )

    @pl.when(step == pl.num_programs(0) - 1)
    def _():
        move_groups(rows, rows_out, 0, count[0], sems)


def move_groups(source, target, to, number, sems):
    depth = sems.shape[0]

    def copy(i):
        return pltpu.make_async_copy(
            source.at[pl.ds(pl.multiple_of(i * LANES, LANES), LANES), :],
            target.at[pl.ds(pl.multiple_of((to + i) * LANES, LANES), LANES), :],
            sems.at[i % depth],
        )

    def start(i, carry):
        @pl.when(i >= depth)
        def _():
            copy(i - depth).wait()

        copy(i).start()
        return carry

    def finish(i, carry):
        copy(i).wait()
        return carry

    lax.fori_loop(0, number, start, 0)
    lax.fori_loop(jnp.maximum(number - depth, 0), number, finish, 0)


def last_kernel(base, earlier, place_ref, bounds_ref, users_ref, keys_ref, weight_ref, *refs):
    tables, before, (solution_ref, resid_ref) = refs[:4], refs[4 : 4 + 5 * earlier], refs[4 + 5 * earlier : 6 + 5 * earlier]
    wide, rows, item_s, weight_s, gram, count, sems = refs[6 + 5 * earlier :]
    step = pl.program_id(0)

    @pl.when(step == 0)
    def _():
        gram[...] = jnp.zeros_like(gram)
        total = 0
        for at in range(earlier):
            rows_ref, item_ref, weight_in, gram_ref, count_ref = before[5 * at : 5 * at + 5]
            number = count_ref[0]
            move_groups(rows_ref, rows, total, number, sems)

            item_s[pl.ds(total, item_ref.shape[0]), :] = item_ref[...]
            weight_s[pl.ds(total, weight_in.shape[0]), :] = weight_in[...]
            gram[...] += gram_ref[...]
            total = total + number
        count[0] = total

    absorb(
        base + step, place_ref, bounds_ref, users_ref, keys_ref, weight_ref,
        pieces_of(tables), wide, rows, item_s, weight_s, gram, count,
    )

    @pl.when(step == pl.num_programs(0) - 1)
    def _():
        solve_items(rows, item_s, weight_s, count, gram, solution_ref, resid_ref)


def solve_items(rows, item_s, weight_s, count, gram, solution_ref, resid_ref):
    groups = STEP // LANES
    filled = count[0]
    steps = (filled + groups - 1) // groups

    def clear(at, carry):
        rows[pl.ds(pl.multiple_of(at * LANES, LANES), LANES), :] = jnp.zeros((LANES, rows.shape[1]), rows.dtype)
        item_s[pl.ds(at, 1), :] = jnp.full((1, LANES), -1, jnp.int32)
        weight_s[pl.ds(at, 1), :] = jnp.zeros((1, LANES), jnp.float32)
        return carry

    lax.fori_loop(filled, steps * groups, clear, 0)
    own = lax.broadcasted_iota(jnp.int32, (ITEM_DEV, STEP), 0)

    def along(ref, step):
        return jnp.concatenate([ref[pl.ds(step * groups + g, 1), :] for g in range(groups)], axis=1)

    def held(step):
        return rows[pl.ds(pl.multiple_of(step * STEP, STEP), STEP), :]

    def halves(pair):
        return pair[:ITEM_DEV] + pair[ITEM_DEV:]

    def summed(term):
        acc = jnp.zeros((2 * ITEM_DEV, rows.shape[1]), jnp.float32)

        done = 0
        for wide in (4, 2, 1):

            def many(i, acc, wide=wide, done=done):
                for k in range(wide):
                    acc = acc + term(done + i * wide + k)
                return acc

            turns = (steps - done) // wide
            acc = lax.fori_loop(0, turns, many, acc)
            done = done + turns * wide
        return halves(acc)

    def rhs_term(step):
        scaled = jnp.where(along(item_s, step) == own, 1.0 + along(weight_s, step), 0.0)
        return jnp.dot(two_parts(scaled), held(step), preferred_element_type=jnp.float32)

    rhs = summed(rhs_term)

    squares = three_parts(gram[...])

    def by_gram(split):
        added = None
        for k, square in enumerate(squares):
            many = jnp.dot(jnp.concatenate(split[: 3 - k], axis=0), square, preferred_element_type=jnp.float32)
            for start in range(0, many.shape[0], ITEM_DEV):
                piece = many[start : start + ITEM_DEV]
                added = piece if added is None else added + piece
        return added

    def image_of(direction):
        split = three_parts(direction)
        parts = jnp.concatenate(split[:2], axis=0)

        def term(step):
            here = held(step)
            dots = lax.dot_general(parts, here, (((1,), (1,)), ((), ())), preferred_element_type=jnp.float32)
            scaled = jnp.where(along(item_s, step) == own, halves(dots) * along(weight_s, step), 0.0)
            return jnp.dot(two_parts(scaled), here, preferred_element_type=jnp.float32)

        return summed(term) + by_gram(split) + REG * direction

    def iterate(_, state):
        solution, resid, direction, norm_now = state
        image = image_of(direction)
        alpha = norm_now / (jnp.sum(direction * image, axis=1, keepdims=True) + EPS)
        solution = solution + alpha * direction
        resid = resid - alpha * image
        norm_next = jnp.sum(resid * resid, axis=1, keepdims=True)
        direction = resid + (norm_next / (norm_now + EPS)) * direction
        return (solution, resid, direction, norm_next)

    state = (jnp.zeros_like(rhs), rhs, rhs, jnp.sum(rhs * rhs, axis=1, keepdims=True))
    solution, resid, _, _ = lax.fori_loop(0, ITERS, iterate, state)
    solution_ref[...] = solution
    resid_ref[...] = resid


def exchange(value, axis, away):
    return lax.ppermute(value, axis, [(i, i ^ away) for i in range(lax.axis_size(axis))])


def tie(value, *others):
    return lax.optimization_barrier((value, *others))[0]


def gathered_body(user_factors, tile_users, tile_items, tile_weight, live_count):
    shard = user_factors[0]
    blocks = lax.axis_size("ublk")
    salts = lax.axis_size("salt")
    tile, rank = shard.shape
    block_users = tile * salts
    slots = tile_users.shape[2]
    lines = slots // LANES
    live = jnp.arange(slots, dtype=jnp.int32) < live_count[0, 0]
    items = tile_items[0, 0]
    key = ((items // ITEM_DEV) * block_users + tile_users[0, 0]) * ITEM_DEV + items % ITEM_DEV
    key = jnp.where(live, key, blocks * block_users * ITEM_DEV)
    key, weight = lax.sort((key, tile_weight[0, 0]), num_keys=1, is_stable=False)
    meta = jnp.stack([key.astype(jnp.float32), weight])[None]
    meta = jnp.concatenate([meta, exchange(meta, "ublk", 1)])
    meta = jnp.concatenate([meta] + [exchange(meta, "ublk", away) for away in range(2, blocks, 2)])
    keys = meta[:, 0].astype(jnp.int32)
    weights = meta[:, 1].reshape(blocks, lines, LANES)
    me = lax.axis_index("ublk").astype(jnp.int32)
    lo = me * (block_users * ITEM_DEV)
    hi = lo + block_users * ITEM_DEV
    bounds = jnp.stack([jnp.sum((keys < lo).astype(jnp.int32), axis=1), jnp.sum((keys < hi).astype(jnp.int32), axis=1)], axis=1)
    users = jnp.clip((keys - lo) // ITEM_DEV, 0, block_users - 1).reshape(blocks, 1, slots)
    place = jnp.stack([me, lax.axis_index("salt").astype(jnp.int32)])
    data = (place, bounds.reshape(-1), users, keys.reshape(blocks, lines, LANES), weights)

    half = tile // 2
    near = []
    own = []

    def specs(base, sets):
        def block_at(i, place_ref, _):
            return (base + i, 0, 0)

        tables = []
        for at in range(sets):
            for _ in range(2):
                for row in range(2):
                    tables.append(
                        pl.BlockSpec((1, tile, rank), lambda i, p, q, at=at, row=row: (2 * row + jnp.clip(i - 2 * at, 0, 1), 0, 0))
                    )
        return [
            pl.BlockSpec((1, 1, slots), block_at, memory_space=pltpu.SMEM),
            pl.BlockSpec((1, lines, LANES), block_at),
            pl.BlockSpec((1, lines, LANES), block_at),
            *tables,
        ]

    def tables_of(start, stop):
        return [part for at in range(start, stop) for part in (own[at], own[at], near[at], near[at])]

    def early(start, stop):
        sets = stop - start
        capacity = 2 * sets * slots
        fixed = lambda i, p, q: (0, 0)
        return pl.pallas_call(
            functools.partial(early_kernel, 2 * start, sets),
            grid_spec=pltpu.PrefetchScalarGridSpec(
                num_scalar_prefetch=2,
                grid=(2 * sets,),
                in_specs=specs(2 * start, sets),
                out_specs=[
                    pl.BlockSpec(memory_space=pl.ANY),
                    pl.BlockSpec((capacity // LANES, LANES), fixed),
                    pl.BlockSpec((capacity // LANES, LANES), fixed),
                    pl.BlockSpec((rank, rank), fixed),
                    pl.BlockSpec(memory_space=pltpu.SMEM),
                ],
                scratch_shapes=[
                    pltpu.VMEM((block_users, rank), jnp.float32),
                    pltpu.VMEM((capacity, rank), jnp.bfloat16),
                    pltpu.SemaphoreType.DMA((8,)),
                ],
            ),
            out_shape=[
                jax.ShapeDtypeStruct((capacity, rank), jnp.bfloat16),
                jax.ShapeDtypeStruct((capacity // LANES, LANES), jnp.int32),
                jax.ShapeDtypeStruct((capacity // LANES, LANES), jnp.float32),
                jax.ShapeDtypeStruct((rank, rank), jnp.float32),
                jax.ShapeDtypeStruct((1,), jnp.int32),
            ],
            compiler_params=pltpu.CompilerParams(vmem_limit_bytes=20 << 20),
            cost_estimate=pl.CostEstimate(flops=sets << 32, bytes_accessed=sets << 23, transcendentals=0),
        )(*data, *tables_of(start, stop))

    far = [shard]
    for away in range(2, blocks, 2):
        far.append(exchange(tie(shard, far[-1]), "ublk", away))
    sets = len(far)
    states = []
    for at, part in enumerate(far):
        if at > 0:
            part = tie(part, beside, above)
        beside = exchange(part, "ublk", 1)
        above = exchange(part, "salt", 2)
        if at >= LAG:
            states.append(early(at - LAG, at - LAG + 1))
            states.append(early(1, 2))
            beside = tie(beside, states[0][4], states[1][4])
            above = tie(above, states[0][4], states[1][4])
        over = exchange(beside[:half], "salt", 2)
        under = exchange(above[half:], "ublk", 1)
        if at < sets - 1:
            mine = jnp.concatenate([part, beside, above, over, under])
            own.append(mine.reshape(salts, tile, rank))
            near.append(exchange(mine, "salt", 1).reshape(salts, tile, rank))
        else:
            most = jnp.concatenate([part, beside, above])
            rest = jnp.concatenate([over, under])
            own.append(jnp.concatenate([most, rest]).reshape(salts, tile, rank))
            near.append(jnp.concatenate([exchange(most, "salt", 1), exchange(rest, "salt", 1)]).reshape(salts, tile, rank))
    for at in range(len(states), sets - 1):
        states.append(early(at, at + 1))

    capacity = blocks * slots + STEP
    out = jax.ShapeDtypeStruct((ITEM_DEV, rank), jnp.float32)
    whole = pl.BlockSpec((ITEM_DEV, rank), lambda i, p, q: (0, 0))
    before_specs = []
    for state in states:
        before_specs += [
            pl.BlockSpec(memory_space=pl.ANY),
            pl.BlockSpec(state[1].shape, lambda i, p, q: (0, 0)),
            pl.BlockSpec(state[2].shape, lambda i, p, q: (0, 0)),
            pl.BlockSpec(state[3].shape, lambda i, p, q: (0, 0)),
            pl.BlockSpec(memory_space=pltpu.SMEM),
        ]
    solution, resid = pl.pallas_call(
        functools.partial(last_kernel, 2 * (sets - 1), len(states)),
        grid_spec=pltpu.PrefetchScalarGridSpec(
            num_scalar_prefetch=2,
            grid=(2,),
            in_specs=specs(2 * (sets - 1), 1) + before_specs,
            out_specs=[whole, whole],
            scratch_shapes=[
                pltpu.VMEM((block_users, rank), jnp.float32),
                pltpu.VMEM((capacity, rank), jnp.bfloat16),
                pltpu.VMEM((capacity // LANES, LANES), jnp.int32),
                pltpu.VMEM((capacity // LANES, LANES), jnp.float32),
                pltpu.VMEM((rank, rank), jnp.float32),
                pltpu.SMEM((1,), jnp.int32),
                pltpu.SemaphoreType.DMA((8,)),
            ],
        ),
        out_shape=[out, out],
        compiler_params=pltpu.CompilerParams(vmem_limit_bytes=32 << 20),
    )(*data, *tables_of(sets - 1, sets), *[part for state in states for part in state])
    return (solution[None], resid[None])


def solution(mesh):
    def body(user_factors, *tiles):
        table_bytes = user_factors.size * mesh.size * user_factors.dtype.itemsize
        blocks = mesh.shape["ublk"]
        swaps = mesh.shape["salt"] == 4 and blocks >= 8 and blocks & (blocks - 1) == 0
        chosen = gathered_body if swaps and table_bytes <= TABLE_BYTES else reduced_body
        return chosen(user_factors, *tiles)

    return jax.shard_map(
        body,
        mesh=mesh,
        in_specs=(
            P("ublk", "salt", None),
            P("ublk", "salt", None),
            P("ublk", "salt", None),
            P("ublk", "salt", None),
            P("ublk", "salt"),
        ),
        out_specs=(P("salt", "ublk", None), P("salt", "ublk", None)),
        check_vma=False,
    )
```
